128 devices in a mesh: gx: 8 (over x, core), gy: 4 (over z), gz: 4 (over y).
Axes of the slice: x: 4, y: 4, z: 4, core: 2. Of those that a mesh axis runs over, the one named last changes fastest.
Arguments:
- source: float32 [128, 256, 512], P('gx', 'gy', 'gz'), may hold values from -5 to 5
- first_guess: float32 [128, 256, 512], P('gx', 'gy', 'gz'), may hold values from -5 to 5
- cell_classes: int32 [128, 256, 512], P('gx', 'gy', 'gz'), may hold values from 0 to 7
- class_table: float32 [8], replicated, may hold values from 0.2 to 5
Outputs:
- solution: float32 [128, 256, 512], P('gx', 'gy', 'gz')
- residual: float32 [128, 256, 512], P('gx', 'gy', 'gz')
The draws below stay inside these ranges and needn't reach their ends.
All inputs are finite; a program needn't handle non-finite values.
Results may differ from the reference program's by a relative error of at most 0.0003.
Values sent between devices are 32-bit elements; how exact they have to be, the bound alone decides.
A program may use at most 192 MiB of HBM per device.

```python
import math
import jax
import jax.numpy as jnp
from jax import lax

LEVELS = 3
SWEEPS = 4
COARSE = 16
CLASSES = 8
NX = 128
NY = 256
NZ = 512


def draw_source(key, part):
    rough = jax.random.normal(key, (NX, NY, NZ), jnp.float32)
    return jnp.clip(rough, -5.0, 5.0)


def place_ends(entries, own_key, low, largest):
    place = [jax.random.randint(jax.random.fold_in(own_key, axis), (), 0, length) for axis, length in enumerate(entries.shape)]
    longest = entries.shape.index(max(entries.shape))
    neighbour = place[:longest] + [(place[longest] + 1) % entries.shape[longest]] + place[longest + 1:]
    return entries.at[tuple(place)].set(low).at[tuple(neighbour)].set(largest)


def shard_levels(own_key, extent, cuts, smallest, high):
    gain, own = 1.0, jax.random.fold_in(own_key, 6)
    for dim, parts in cuts:
        draws = jnp.exp(jax.random.uniform(jax.random.fold_in(own, dim), (parts,), jnp.float32, smallest / len(cuts), high / len(cuts)))
        gain = gain * jnp.repeat(draws, extent[dim] // parts).reshape([-1 if axis == dim else 1 for axis in range(len(extent))])
    return gain


def gaussian(rng, dims, scale, most, cuts=(), kind=jnp.bfloat16):
    array = jax.random.normal(rng, dims, jnp.float32) * scale
    if len(cuts) > 0:
        array = shard_levels(rng, dims, cuts, -0.22, 0.18) * array
    return jnp.clip(array, min=-most, max=most).astype(kind)


def setup_inputs(seed: int = 0) -> dict:
    keys = jax.random.split(jax.random.key(seed), 5)
    source = draw_source(jax.random.fold_in(keys[4], 71), 0)
    first_guess = gaussian(keys[1], (NX, NY, NZ), 1.0, 5.0, ((0, 8), (1, 4), (2, 4)), jnp.float32)
    cell_classes = place_ends(jax.random.randint(keys[2], (NX, NY, NZ), 0, CLASSES), jax.random.fold_in(keys[2], 1), 0, CLASSES - 1).astype(jnp.int32)
    class_table = jnp.clip(jnp.exp(jax.random.uniform(keys[3], (CLASSES,), jnp.float32, math.log(0.2), math.log(5.0))), 0.2, 5.0)
    return dict(source=source, first_guess=first_guess, cell_classes=cell_classes, class_table=class_table)


relax_weight = 0.85


def neighbor(padded, axis_dim, offset):
    window = [slice(1, -1), slice(1, -1), slice(1, -1)]
    window[axis_dim] = slice(1 + offset, padded.shape[axis_dim] - 1 + offset)
    return padded[tuple(window)]


def apply_padded(padded_u, padded_c, level_scale):
    center_u = padded_u[1:-1, 1:-1, 1:-1]
    center_c = padded_c[1:-1, 1:-1, 1:-1]
    stencil_sum = jnp.zeros_like(center_u)
    diagonal = jnp.zeros_like(center_u)
    for axis_dim in range(3):
        for offset in (-1, 1):
            face = 0.5 * (center_c + neighbor(padded_c, axis_dim, offset))
            stencil_sum = stencil_sum + face * (center_u - neighbor(padded_u, axis_dim, offset))
            diagonal = diagonal + face
    return level_scale * stencil_sum, level_scale * diagonal


def restrict(field):
    size_x, size_y, size_z = field.shape
    return field.reshape(size_x // 2, 2, size_y // 2, 2, size_z // 2, 2).mean(axis=(1, 3, 5))


def prolong(field):
    size_x, size_y, size_z = field.shape
    spread = jnp.broadcast_to(field[:, None, :, None, :, None], (size_x, 2, size_y, 2, size_z, 2))
    return spread.reshape(2 * size_x, 2 * size_y, 2 * size_z)


def sweep(values, rhs_field, coef_padded, level_scale):
    stencil_sum, diagonal = apply_padded(jnp.pad(values, 1), coef_padded, level_scale)
    return values + relax_weight * (rhs_field - stencil_sum) / diagonal


def residual_of(values, rhs_field, coef_padded, level_scale):
    stencil_sum, diagonal = apply_padded(jnp.pad(values, 1), coef_padded, level_scale)
    return rhs_field - stencil_sum


def reference(source, first_guess, cell_classes, class_table):
    coef_list = [class_table[cell_classes]]
    for level_id in range(LEVELS):
        coef_list.append(restrict(coef_list[-1]))
    padded_list = [jnp.pad(coef_value, 1) for coef_value in coef_list]
    rhs_list = [source]
    iterate_list = []
    values = first_guess
    for level_id in range(LEVELS):
        level_scale = 0.25 ** level_id
        if level_id > 0:
            values = jnp.zeros_like(rhs_list[level_id])
        for sweep_id in range(SWEEPS):
            values = sweep(values, rhs_list[level_id], padded_list[level_id], level_scale)
        iterate_list.append(values)
        rhs_list.append(restrict(residual_of(values, rhs_list[level_id], padded_list[level_id], level_scale)))
    coarse_scale = 0.25 ** LEVELS
    coarse_rhs = rhs_list[LEVELS]
    coarse_pad = padded_list[LEVELS]

    def coarse_step(sweep_id, values):
        return sweep(values, coarse_rhs, coarse_pad, coarse_scale)

    correction = lax.fori_loop(0, COARSE, coarse_step, jnp.zeros_like(coarse_rhs))
    for level_id in reversed(range(LEVELS)):
        level_scale = 0.25 ** level_id
        values = iterate_list[level_id] + prolong(correction)
        for sweep_id in range(SWEEPS):
            values = sweep(values, rhs_list[level_id], padded_list[level_id], level_scale)
        correction = values
    final = residual_of(correction, source, padded_list[0], 1.0)
    return correction, final
```

```python
import functools

import jax
import jax.numpy as jnp
from jax import lax
from jax.experimental import pallas as pl
from jax.experimental.pallas import tpu as pltpu
from jax.sharding import PartitionSpec as P

LEVELS = 3
SWEEPS = 4
COARSE = 16
WEIGHT = 0.85
LANES = 128
PAD = 8
MESH = pl.DeviceIdType.MESH
HIGHEST = lax.Precision.HIGHEST


class Level:
    def __init__(self, index, shape, refs):
        self.index = index
        self.planes, self.rows, self.width = shape
        self.pitch = self.rows + 2 * PAD
        self.scale = 0.25**index
        self.packed = max(self.planes, 8)
        for name, ref in refs.items():
            setattr(self, name, ref)

    def row(self, slot, plane):
        return (slot * (self.planes + 2) + plane) * self.pitch + PAD


def level_scratch(shape):
    planes, rows, _ = shape
    f32 = jnp.float32
    packed = max(planes, 8)
    flat = planes * rows
    return dict(
        v=pltpu.VMEM((3 * (planes + 2) * (rows + 2 * PAD), LANES), f32),
        ysend=pltpu.VMEM((3 * 2 * packed, LANES), f32),
        yrecv=pltpu.VMEM((3 * 2 * packed, LANES), f32),
        zsend=pltpu.VMEM((3 * rows, LANES), f32),
        zrecv=pltpu.VMEM((3 * 2 * rows, LANES), f32),
        edge=pltpu.VMEM((rows, LANES), f32),
        off=pltpu.VMEM((6 * flat, LANES), f32),
        rhs=pltpu.VMEM((flat, LANES), f32),
        inverse=pltpu.VMEM((flat, LANES), f32),
        diag=pltpu.VMEM((flat, LANES), f32),
        res=pltpu.VMEM((flat, LANES), f32),
        half=pltpu.VMEM((max(flat // 4, 8), LANES), f32),
        send=pltpu.SemaphoreType.DMA((3, 6)),
        recv=pltpu.SemaphoreType.DMA((3, 6)),
    )


def lanes_of(rows):
    return lax.broadcasted_iota(jnp.int32, (rows, LANES), 1)


def pack(level, plane, values, held):
    lane = lanes_of(level.rows)
    first = 2 * plane + 1
    mask = (lane == first) | (lane == ((first + level.width - 1) & (LANES - 1)))
    return jnp.where(mask, pltpu.roll(values, first, 1), held)


def push(level, slot, held, around):
    planes, rows, packed = level.planes, level.rows, level.packed
    level.zsend[pl.ds(slot * rows, rows), :] = held
    for side, row in ((0, 0), (1, rows - 1)):
        level.ysend[pl.ds((slot * 2 + side) * packed, planes), :] = level.v[
            pl.ds(level.row(slot, 1) + row, planes, stride=level.pitch), :
        ]
    own = lambda plane: level.v.at[pl.ds(level.row(slot, plane), rows), :]
    ysend = lambda side: level.ysend.at[pl.ds((slot * 2 + side) * packed, packed), :]
    yrecv = lambda side: level.yrecv.at[pl.ds((slot * 2 + side) * packed, packed), :]
    zsend = level.zsend.at[pl.ds(slot * rows, rows), :]
    zrecv = lambda side: level.zrecv.at[pl.ds((slot * 2 + side) * rows, rows), :]
    plan = (
        (own(planes), own(0), "gx", 1),
        (own(1), own(planes + 1), "gx", -1),
        (ysend(1), yrecv(0), "gy", 1),
        (ysend(0), yrecv(1), "gy", -1),
        (zsend, zrecv(0), "gz", 1),
        (zsend, zrecv(1), "gz", -1),
    )
    copies = []
    for number, (src, dst, axis, step) in enumerate(plan):
        copy = pltpu.make_async_remote_copy(
            src_ref=src,
            dst_ref=dst,
            send_sem=level.send.at[slot, number],
            recv_sem=level.recv.at[slot, number],
            device_id=around(axis, step),
            device_id_type=MESH,
        )
        copy.start()
        copies.append(copy)
    return copies


def pull(level, slot, copies):
    planes, rows, packed, width = level.planes, level.rows, level.packed, level.width
    for copy in copies:
        copy.wait()
    for side, row in ((0, -1), (1, rows)):
        level.v[pl.ds(level.row(slot, 1) + row, planes, stride=level.pitch), :] = level.yrecv[
            pl.ds((slot * 2 + side) * packed, planes), :
        ]
    below = level.zrecv[pl.ds(slot * 2 * rows, rows), :]
    above = level.zrecv[pl.ds((slot * 2 + 1) * rows, rows), :]
    if width < LANES:
        below = pltpu.roll(below, LANES - width, 1)
    above = pltpu.roll(above, width - 2, 1)
    level.edge[...] = jnp.where((lanes_of(rows) & 1) == 0, below, above)


def neighbours(level, slot, plane, center):
    rows, width = level.rows, level.width
    first = level.row(slot, 1) + plane * level.pitch
    at = lambda shift: level.v[pl.ds(first + shift, rows), :]
    lane = lanes_of(rows)
    edge = pltpu.roll(level.edge[...], (LANES - 2 * plane) & (LANES - 1), 1)
    return (
        at(-level.pitch),
        at(level.pitch),
        at(-1),
        at(1),
        jnp.where(lane == 0, edge, pltpu.roll(center, 1, 1)),
        jnp.where(lane == width - 1, edge, pltpu.roll(center, LANES - 1, 1)),
    )


def change(level, slot, plane):
    rows, flat = level.rows, level.planes * level.rows
    center = level.v[pl.ds(level.row(slot, 1) + plane * level.pitch, rows), :]
    total = level.rhs[pl.ds(plane * rows, rows), :] - WEIGHT * center
    for number, value in enumerate(neighbours(level, slot, plane, center)):
        total = total + level.off[pl.ds(number * flat + plane * rows, rows), :] * value
    return center, total


def sweep(level, slot, last=False):
    def step(plane, held):
        center, total = change(level, slot, plane)
        new = center + total
        level.v[pl.ds(level.row(1 - slot, 1) + plane * level.pitch, level.rows), :] = new
        return held if last else pack(level, plane, new, held)

    return lax.fori_loop(0, level.planes, step, jnp.zeros((level.rows, LANES), jnp.float32))


def residual(level, slot, out):
    def step(plane, _):
        at = pl.ds(plane * level.rows, level.rows)
        out[at, :] = change(level, slot, plane)[1] * level.diag[at, :]
        return 0

    lax.fori_loop(0, level.planes, step, 0)


def smooth(level, slot, held, around, count):
    for _ in range(count):
        pull(level, slot, push(level, slot, held, around))
        held = sweep(level, slot)
        slot = 1 - slot
    return slot, held


def restrict(level, ref, first, pitch):
    size = level.rows // 2
    for plane in range(level.planes // 2):
        parts = [
            ref[pl.ds(first + (2 * plane + p) * pitch + q, size, stride=2), :]
            for p in range(2)
            for q in range(2)
        ]
        level.half[pl.ds(plane * size, size), :] = (parts[0] + parts[1]) + (parts[2] + parts[3])
    row = lax.broadcasted_iota(jnp.int32, (LANES, LANES), 0)
    column = lax.broadcasted_iota(jnp.int32, (LANES, LANES), 1)
    gather = jnp.where((row >> 1) == column, 0.125, 0.0)
    return lax.dot(level.half[...], gather, precision=HIGHEST, preferred_element_type=jnp.float32)


def prolong(level, slot, coarse):
    row = lax.broadcasted_iota(jnp.int32, (LANES, LANES), 0)
    column = lax.broadcasted_iota(jnp.int32, (LANES, LANES), 1)
    spread = jnp.where(row == (column >> 1), 1.0, 0.0)
    level.half[...] = lax.dot(coarse, spread, precision=HIGHEST, preferred_element_type=jnp.float32)
    size = level.rows // 2
    held = jnp.zeros((level.rows, LANES), jnp.float32)
    for plane in range(level.planes):
        parent = level.half[pl.ds((plane // 2) * size, size), :]
        old, new = level.row(slot, plane + 1), level.row(1 - slot, plane + 1)
        for q in range(2):
            level.v[pl.ds(new + q, size, stride=2), :] = (
                level.v[pl.ds(old + q, size, stride=2), :] + parent
            )
        held = pack(level, plane, level.v[pl.ds(new, level.rows), :], held)
    return held


def put(level, slot, values):
    held = jnp.zeros((level.rows, LANES), jnp.float32)
    for plane in range(level.planes):
        part = values[plane * level.rows : (plane + 1) * level.rows, :]
        level.v[pl.ds(level.row(slot, plane + 1), level.rows), :] = part
        held = pack(level, plane, part, held)
    return held


def coefficients(level, ends):
    rows, planes, width, flat = level.rows, level.planes, level.width, level.planes * level.rows
    lane = lanes_of(rows)
    row = lax.broadcasted_iota(jnp.int32, (rows, LANES), 0)

    def step(plane, _):
        center = level.v[pl.ds(level.row(2, 1) + plane * level.pitch, rows), :]
        outside = (
            ((row >= 0) & (plane == 0)) & (ends["gx"][0]),
            ((row >= 0) & (plane == planes - 1)) & (ends["gx"][1]),
            (row == 0) & ends["gy"][0],
            (row == rows - 1) & ends["gy"][1],
            (lane == 0) & ends["gz"][0],
            (lane == width - 1) & ends["gz"][1],
        )
        faces = [
            0.5 * (center + jnp.where(out, 0.0, value))
            for out, value in zip(outside, neighbours(level, 2, plane, center), strict=True)
        ]
        diagonal = sum(faces[1:], faces[0])
        inverse = jnp.where(lane < width, WEIGHT / diagonal, 0.0)
        at = pl.ds(plane * rows, rows)
        level.inverse[at, :] = inverse * (1.0 / level.scale)
        level.diag[at, :] = diagonal * (level.scale / WEIGHT)
        for number in range(6):
            level.off[pl.ds(number * flat + plane * rows, rows), :] = jnp.where(
                outside[number], 0.0, faces[number] * inverse
            )
        return 0

    lax.fori_loop(0, planes, step, 0)


def gather_ring(field, which, co, place, around):
    rows = field.shape[0] // 2
    tile = pltpu.roll(field[:rows, :], place["lane"], 1) + pltpu.roll(
        field[rows:, :], place["lane"] + LANES // 2, 1
    )
    co["tile"][pl.ds(which * 8, 8), :] = tile
    copies = []
    for step in range(1, place["count"]["gz"]):
        copy = pltpu.make_async_remote_copy(
            src_ref=co["tile"].at[pl.ds(which * 8, 8), :],
            dst_ref=co["tiles"].at[pl.ds((which * 4 + step) * 8, 8), :],
            send_sem=co["ring_send"].at[which, step],
            recv_sem=co["ring_recv"].at[which, step],
            device_id=around("gz", step),
            device_id_type=MESH,
        )
        copy.start()
        copies.append(copy)
    return tile, copies


def gather_plane(tile, copies, which, co, place, around):
    for copy in copies:
        copy.wait()
    for step in range(1, place["count"]["gz"]):
        tile = tile + co["tiles"][pl.ds((which * 4 + step) * 8, 8), :]
    mine = co["whole"].at[which, pl.ds(place["row"], 8), :]
    mine[...] = tile
    for along in range(place["count"]["gx"]):
        for across in range(place["count"]["gy"]):
            if along == 0 and across == 0:
                continue
            pltpu.make_async_remote_copy(
                src_ref=mine,
                dst_ref=mine,
                send_sem=co["plane_send"].at[which],
                recv_sem=co["plane_recv"].at[which],
                device_id={**around("gx", along), **around("gy", across)},
                device_id_type=MESH,
            ).start()


def gather_wait(which, co):
    total = co["whole"].shape[1]
    others = co["whole"].at[which, pl.ds(0, total - 8), :]
    pltpu.make_async_copy(others, others, co["plane_send"].at[which]).wait()
    pltpu.make_async_copy(others, others, co["plane_recv"].at[which]).wait()


def coarse_solve(co, scale):
    total = co["whole"].shape[1]
    count, rows = co["whole"].shape[1] // 32, 32
    lane = lanes_of(rows)
    row = lax.broadcasted_iota(jnp.int32, (rows, LANES), 0)
    low = lane < LANES // 2
    depth = lane & (LANES // 2 - 1)

    def around_of(read, group):
        center = read(group)
        swap = lambda g: pltpu.roll(read(g), LANES // 2, 1)
        here = swap(group)
        before = swap(group - 1) if group > 0 else here
        after = swap(group + 1) if group < count - 1 else here
        return center, (
            jnp.where(low, before, here),
            jnp.where(low, here, after),
            pltpu.roll(center, 1, 0),
            pltpu.roll(center, rows - 1, 0),
            pltpu.roll(center, 1, 1),
            pltpu.roll(center, LANES - 1, 1),
        )

    read_coef = lambda g: co["whole"][0, pl.ds(g * rows, rows), :]
    for group in range(count):
        center, values = around_of(read_coef, group)
        never = row < 0
        outside = (
            low if group == 0 else never,
            ~low if group == count - 1 else never,
            row == 0,
            row == rows - 1,
            depth == 0,
            depth == LANES // 2 - 1,
        )
        faces = [
            0.5 * (center + jnp.where(out, 0.0, value))
            for out, value in zip(outside, values, strict=True)
        ]
        diagonal = sum(faces[1:], faces[0])
        inverse = WEIGHT / diagonal
        at = pl.ds(group * rows, rows)
        for number in range(6):
            co["off"][number, at, :] = jnp.where(outside[number], 0.0, faces[number] * inverse)
        co["inverse"][at, :] = inverse * (1.0 / scale)

    yield

    start = co["whole"][1] * co["inverse"][...]
    co["inverse"][...] = start
    co["v"][0] = jnp.zeros((total, LANES), jnp.float32)

    def one(slot):
        read = lambda g: co["v"][slot, pl.ds(g * rows, rows), :]
        for group in range(count):
            center, values = around_of(read, group)
            at = pl.ds(group * rows, rows)
            new = co["inverse"][at, :] + (1.0 - WEIGHT) * center
            for number, value in enumerate(values):
                new = new + co["off"][number, at, :] * value
            co["v"][1 - slot, at, :] = new

    def pair(_, carry):
        one(0)
        one(1)
        return carry

    lax.fori_loop(0, COARSE // 2, pair, 0)


def kernel(shapes, counts, table, source, guess, classes, out_u, out_r, refs, co):
    levels = [Level(index, shape, ref) for index, (shape, ref) in enumerate(zip(shapes, refs, strict=True))]
    top = levels[0]
    position = {axis: lax.axis_index(axis) for axis in counts}

    def around(axis, step):
        count = counts[axis]
        return {axis: lax.rem(position[axis] + (step + count), count)}

    ends = {axis: (position[axis] == 0, position[axis] == counts[axis] - 1) for axis in counts}
    piece = shapes[-1][2] // 2
    place = dict(
        count=counts,
        lane=position["gz"] * piece,
        row=pl.multiple_of(position["gx"] * 32 + position["gy"] * 8, 8),
    )

    barrier = pltpu.get_barrier_semaphore()
    met = 0
    for along in range(counts["gx"]):
        for across in range(counts["gy"]):
            if along or across:
                where = {**around("gx", along), **around("gy", across)}
                pl.semaphore_signal(barrier, inc=1, device_id=where, device_id_type=MESH)
                met += 1
    for step in range(1, counts["gz"]):
        pl.semaphore_signal(barrier, inc=1, device_id=around("gz", step), device_id_type=MESH)
        met += 1

    entries = [table[k] for k in range(8)]

    def begin(plane, carry):
        held_c, held_v = carry
        at = pl.ds(plane * top.rows, top.rows)
        kind = classes[at, :]
        bits = [(kind & (1 << k)) != 0 for k in range(3)]
        pick = entries
        for bit in bits:
            pick = [jnp.where(bit, pick[2 * k + 1], pick[2 * k]) for k in range(len(pick) // 2)]
        coef = pick[0]
        values = guess[at, :]
        top.v[pl.ds(top.row(2, 1) + plane * top.pitch, top.rows), :] = coef
        top.v[pl.ds(top.row(0, 1) + plane * top.pitch, top.rows), :] = values
        return pack(top, plane, coef, held_c), pack(top, plane, values, held_v)

    for level in levels:
        level.ysend[...] = jnp.zeros_like(level.ysend)
    empty = jnp.zeros((top.rows, LANES), jnp.float32)
    held_c, held_v = lax.fori_loop(0, top.planes, begin, (empty, empty))
    pl.semaphore_wait(barrier, met)

    moving = [push(top, 2, held_c, around)]
    first = push(top, 0, held_v, around)
    for level, below in zip(levels, levels[1:]):
        coarse = restrict(level, level.v, level.row(2, 1), level.pitch)
        moving.append(push(below, 2, put(below, 2, coarse), around))
    last = levels[-1]
    coarse = restrict(last, last.v, last.row(2, 1), last.pitch)
    tile, copies = gather_ring(coarse, 0, co, place, around)
    for level, copy in zip(levels, moving):
        pull(level, 2, copy)
        coefficients(level, ends)
    gather_plane(tile, copies, 0, co, place, around)

    top.rhs[...] = source[...] * top.inverse[...]
    pull(top, 0, first)
    held = sweep(top, 0)
    slot, held = smooth(top, 1, held, around, SWEEPS - 1)
    slots = []
    for level, below in zip(levels, levels[1:] + [None]):
        pull(level, slot, push(level, slot, held, around))
        residual(level, slot, level.res)
        slots.append(slot)
        rhs = restrict(level, level.res, 0, level.rows)
        if below is not None:
            start = rhs * below.inverse[...]
            below.rhs[...] = start
            held = put(below, 0, start)
            slot, held = smooth(below, 0, held, around, SWEEPS - 1)

    tile, copies = gather_ring(rhs, 1, co, place, around)
    gather_plane(tile, copies, 1, co, place, around)
    gather_wait(0, co)
    solve = coarse_solve(co, 0.25**LEVELS)
    next(solve)
    gather_wait(1, co)
    next(solve, None)

    mine = co["v"][0, pl.ds(place["row"], 8), :]
    inside = lanes_of(8) < piece
    back = LANES - place["lane"]
    coarse = jnp.concatenate(
        [
            jnp.where(inside, pltpu.roll(mine, back & (LANES - 1), 1), 0.0),
            jnp.where(inside, pltpu.roll(mine, (back + LANES // 2) & (LANES - 1), 1), 0.0),
        ],
        axis=0,
    )
    for level in reversed(levels):
        slot = slots[level.index]
        held = prolong(level, slot, coarse)
        slot, held = smooth(level, 1 - slot, held, around, SWEEPS)
        if level.index > 0:
            coarse = jnp.concatenate(
                [level.v[pl.ds(level.row(slot, plane + 1), level.rows), :] for plane in range(level.planes)],
                axis=0,
            )
    copies = push(top, slot, held, around)
    for plane in range(top.planes):
        out_u[pl.ds(plane * top.rows, top.rows), :] = top.v[pl.ds(top.row(slot, plane + 1), top.rows), :]
    pull(top, slot, copies)
    residual(top, slot, out_r)


def body(counts, source, first_guess, cell_classes, class_table):
    planes, rows, width = source.shape
    shapes = [(planes >> k, rows >> k, width >> k) for k in range(LEVELS)]
    flat = (planes * rows, width)
    whole = counts["gx"] * 32
    f32 = jnp.float32
    co = dict(
        tile=pltpu.VMEM((2 * 8, LANES), f32),
        tiles=pltpu.VMEM((2 * 4 * 8, LANES), f32),
        whole=pltpu.VMEM((2, whole, LANES), f32),
        off=pltpu.VMEM((6, whole, LANES), f32),
        inverse=pltpu.VMEM((whole, LANES), f32),
        v=pltpu.VMEM((2, whole, LANES), f32),
        ring_send=pltpu.SemaphoreType.DMA((2, 4)),
        ring_recv=pltpu.SemaphoreType.DMA((2, 4)),
        plane_send=pltpu.SemaphoreType.DMA((2,)),
        plane_recv=pltpu.SemaphoreType.DMA((2,)),
    )
    vmem = pl.BlockSpec(memory_space=pltpu.VMEM)
    solution_out, residual_out = pl.pallas_call(
        functools.partial(kernel, shapes, counts),
        out_shape=[jax.ShapeDtypeStruct(flat, f32)] * 2,
        in_specs=[pl.BlockSpec(memory_space=pltpu.SMEM), vmem, vmem, vmem],
        out_specs=[vmem, vmem],
        scratch_shapes=[[level_scratch(shape) for shape in shapes], co],
        compiler_params=pltpu.CompilerParams(
            collective_id=0, has_side_effects=True, vmem_limit_bytes=48 * 1024 * 1024
        ),
        cost_estimate=pl.CostEstimate(flops=100_000_000, bytes_accessed=3_000_000, transcendentals=0),
        name="vcycle",
    )(class_table, source.reshape(flat), first_guess.reshape(flat), cell_classes.reshape(flat))
    return solution_out.reshape(source.shape), residual_out.reshape(source.shape)


def solution(mesh):
    counts = {axis: mesh.shape[axis] for axis in ("gx", "gy", "gz")}
    spec = P("gx", "gy", "gz")
    return jax.shard_map(
        functools.partial(body, counts),
        mesh=mesh,
        in_specs=(spec, spec, spec, P()),
        out_specs=(spec, spec),
        check_vma=False,
    )
```

```python
import functools

import jax
import jax.numpy as jnp
from jax import lax
from jax.experimental import pallas as pl
from jax.experimental.pallas import tpu as pltpu
from jax.sharding import PartitionSpec as P

LEVELS = 3
SWEEPS = 4
COARSE = 16
WEIGHT = 0.85
LANES = 128
PAD = 8
HALO = 4
MESH = pl.DeviceIdType.MESH
HIGHEST = lax.Precision.HIGHEST


class Level:
    def __init__(self, index, shape, refs):
        self.index = index
        self.planes, self.rows, self.width = shape
        self.pitch = self.rows + 2 * PAD
        self.scale = 0.25**index
        self.packed = max(self.planes, 8)
        for name, ref in refs.items():
            setattr(self, name, ref)

    def row(self, slot, plane):
        return (slot * (self.planes + 2) + plane) * self.pitch + PAD


def level_scratch(shape):
    planes, rows, _ = shape
    f32 = jnp.float32
    packed = max(planes, 8)
    flat = planes * rows
    return dict(
        v=pltpu.VMEM((3 * (planes + 2) * (rows + 2 * PAD), LANES), f32),
        ysend=pltpu.VMEM((3 * 2 * packed, LANES), f32),
        yrecv=pltpu.VMEM((3 * 2 * packed, LANES), f32),
        zsend=pltpu.VMEM((3 * rows, LANES), f32),
        zrecv=pltpu.VMEM((3 * 2 * rows, LANES), f32),
        edge=pltpu.VMEM((rows, LANES), f32),
        off=pltpu.VMEM((6 * flat, LANES), f32),
        rhs=pltpu.VMEM((flat, LANES), f32),
        inverse=pltpu.VMEM((flat, LANES), f32),
        diag=pltpu.VMEM((flat, LANES), f32),
        res=pltpu.VMEM((flat, LANES), f32),
        half=pltpu.VMEM((max(flat // 4, 8), LANES), f32),
        send=pltpu.SemaphoreType.DMA((3, 6)),
        recv=pltpu.SemaphoreType.DMA((3, 6)),
    )


def lanes_of(rows):
    return lax.broadcasted_iota(jnp.int32, (rows, LANES), 1)


def pack(level, plane, values, held):
    lane = lanes_of(level.rows)
    first = 2 * plane + 1
    mask = (lane == first) | (lane == ((first + level.width - 1) & (LANES - 1)))
    return jnp.where(mask, pltpu.roll(values, first, 1), held)


def push(level, slot, held, around):
    planes, rows, packed = level.planes, level.rows, level.packed
    level.zsend[pl.ds(slot * rows, rows), :] = held
    for side, row in ((0, 0), (1, rows - 1)):
        level.ysend[pl.ds((slot * 2 + side) * packed, planes), :] = level.v[
            pl.ds(level.row(slot, 1) + row, planes, stride=level.pitch), :
        ]
    own = lambda plane: level.v.at[pl.ds(level.row(slot, plane), rows), :]
    ysend = lambda side: level.ysend.at[pl.ds((slot * 2 + side) * packed, packed), :]
    yrecv = lambda side: level.yrecv.at[pl.ds((slot * 2 + side) * packed, packed), :]
    zsend = level.zsend.at[pl.ds(slot * rows, rows), :]
    zrecv = lambda side: level.zrecv.at[pl.ds((slot * 2 + side) * rows, rows), :]
    plan = (
        (own(planes), own(0), "gx", 1),
        (own(1), own(planes + 1), "gx", -1),
        (ysend(1), yrecv(0), "gy", 1),
        (ysend(0), yrecv(1), "gy", -1),
        (zsend, zrecv(0), "gz", 1),
        (zsend, zrecv(1), "gz", -1),
    )
    copies = []
    for number, (src, dst, axis, step) in enumerate(plan):
        copy = pltpu.make_async_remote_copy(
            src_ref=src,
            dst_ref=dst,
            send_sem=level.send.at[slot, number],
            recv_sem=level.recv.at[slot, number],
            device_id=around(axis, step),
            device_id_type=MESH,
        )
        copy.start()
        copies.append(copy)
    return copies


def pull(level, slot, copies):
    planes, rows, packed, width = level.planes, level.rows, level.packed, level.width
    for copy in copies:
        copy.wait()
    for side, row in ((0, -1), (1, rows)):
        level.v[pl.ds(level.row(slot, 1) + row, planes, stride=level.pitch), :] = level.yrecv[
            pl.ds((slot * 2 + side) * packed, planes), :
        ]
    below = level.zrecv[pl.ds(slot * 2 * rows, rows), :]
    above = level.zrecv[pl.ds((slot * 2 + 1) * rows, rows), :]
    if width < LANES:
        below = pltpu.roll(below, LANES - width, 1)
    above = pltpu.roll(above, width - 2, 1)
    level.edge[...] = jnp.where((lanes_of(rows) & 1) == 0, below, above)


def neighbours(level, slot, plane, center):
    rows, width = level.rows, level.width
    first = level.row(slot, 1) + plane * level.pitch
    at = lambda shift: level.v[pl.ds(first + shift, rows), :]
    lane = lanes_of(rows)
    edge = pltpu.roll(level.edge[...], (LANES - 2 * plane) & (LANES - 1), 1)
    return (
        at(-level.pitch),
        at(level.pitch),
        at(-1),
        at(1),
        jnp.where(lane == 0, edge, pltpu.roll(center, 1, 1)),
        jnp.where(lane == width - 1, edge, pltpu.roll(center, LANES - 1, 1)),
    )


def change(level, slot, plane):
    rows, flat = level.rows, level.planes * level.rows
    center = level.v[pl.ds(level.row(slot, 1) + plane * level.pitch, rows), :]
    total = level.rhs[pl.ds(plane * rows, rows), :] - WEIGHT * center
    for number, value in enumerate(neighbours(level, slot, plane, center)):
        total = total + level.off[pl.ds(number * flat + plane * rows, rows), :] * value
    return center, total


def sweep(level, slot):
    held = jnp.zeros((level.rows, LANES), jnp.float32)
    for plane in range(level.planes):
        center, total = change(level, slot, plane)
        new = center + total
        level.v[pl.ds(level.row(1 - slot, 1) + plane * level.pitch, level.rows), :] = new
        held = pack(level, plane, new, held)
    return held


def residual(level, slot, out):
    for plane in range(level.planes):
        at = pl.ds(plane * level.rows, level.rows)
        out[at, :] = change(level, slot, plane)[1] * level.diag[at, :]


def smooth(level, slot, held, around, count, between=()):
    between = list(between)
    for _ in range(count):
        copies = push(level, slot, held, around)
        if between:
            between.pop(0)()
        pull(level, slot, copies)
        held = sweep(level, slot)
        slot = 1 - slot
    return slot, held


def restrict(level, read):
    size = level.rows // 2
    for plane in range(level.planes // 2):
        parts = [read(2 * plane + p, q, size) for p in range(2) for q in range(2)]
        level.half[pl.ds(plane * size, size), :] = (parts[0] + parts[1]) + (parts[2] + parts[3])
    row = lax.broadcasted_iota(jnp.int32, (LANES, LANES), 0)
    column = lax.broadcasted_iota(jnp.int32, (LANES, LANES), 1)
    gather = jnp.where((row >> 1) == column, 0.125, 0.0)
    return lax.dot(level.half[...], gather, precision=HIGHEST, preferred_element_type=jnp.float32)


def spread(level, coarse):
    row = lax.broadcasted_iota(jnp.int32, (LANES, LANES), 0)
    column = lax.broadcasted_iota(jnp.int32, (LANES, LANES), 1)
    twice = jnp.where(row == (column >> 1), 1.0, 0.0)
    level.half[...] = lax.dot(coarse, twice, precision=HIGHEST, preferred_element_type=jnp.float32)


def prolong(level, slot, coarse):
    spread(level, coarse)
    size = level.rows // 2
    held = jnp.zeros((level.rows, LANES), jnp.float32)
    for plane in range(level.planes):
        parent = level.half[pl.ds((plane // 2) * size, size), :]
        old, new = level.row(slot, plane + 1), level.row(1 - slot, plane + 1)
        for q in range(2):
            level.v[pl.ds(new + q, size, stride=2), :] = (
                level.v[pl.ds(old + q, size, stride=2), :] + parent
            )
        held = pack(level, plane, level.v[pl.ds(new, level.rows), :], held)
    return held


def coefficients(level, ends):
    rows, planes, width, flat = level.rows, level.planes, level.width, level.planes * level.rows
    lane = lanes_of(rows)
    row = lax.broadcasted_iota(jnp.int32, (rows, LANES), 0)

    never = row < 0
    for plane in range(planes):
        center = level.v[pl.ds(level.row(2, 1) + plane * level.pitch, rows), :]
        outside = (
            ends["gx"][0] if plane == 0 else never,
            ends["gx"][1] if plane == planes - 1 else never,
            (row == 0) & ends["gy"][0],
            (row == rows - 1) & ends["gy"][1],
            (lane == 0) & ends["gz"][0],
            (lane == width - 1) & ends["gz"][1],
        )
        faces = [
            0.5 * (center + jnp.where(out, 0.0, value))
            for out, value in zip(outside, neighbours(level, 2, plane, center), strict=True)
        ]
        diagonal = sum(faces[1:], faces[0])
        inverse = WEIGHT / diagonal
        at = pl.ds(plane * rows, rows)
        level.inverse[at, :] = inverse
        level.diag[at, :] = diagonal * (1.0 / WEIGHT)
        for number in range(6):
            level.off[pl.ds(number * flat + plane * rows, rows), :] = jnp.where(
                outside[number], 0.0, faces[number] * inverse
            )


class Wide:
    def __init__(self, index, shape, refs):
        self.index = index
        self.planes, self.rows, self.width = shape
        self.tall = self.rows + 2 * PAD
        self.scale = 0.25**index
        for name, ref in refs.items():
            setattr(self, name, ref)


COEF, RHS, AFTER = 2, 3, 4


def wide_scratch(shape):
    planes, rows, _ = shape
    f32 = jnp.float32
    deep, tall = planes + 2 * HALO, rows + 2 * PAD
    return dict(
        v=pltpu.VMEM((5, deep, tall + 2 * PAD, LANES), f32),
        ends=pltpu.VMEM((3, rows, LANES), f32),
        met=pltpu.VMEM((3, 2, 3, tall, LANES), f32),
        off=pltpu.VMEM((6, deep, tall, LANES), f32),
        inverse=pltpu.VMEM((planes * rows, LANES), f32),
        diag=pltpu.VMEM((planes * rows, LANES), f32),
        res=pltpu.VMEM((planes * rows, LANES), f32),
        half=pltpu.VMEM((planes * rows // 4, LANES), f32),
        send=pltpu.SemaphoreType.DMA((3, 27)),
        recv=pltpu.SemaphoreType.DMA((3, 27)),
    )


def wide_push(level, slot, around):
    planes, rows, width, turn = level.planes, level.rows, level.width, slot - 2
    lane = lanes_of(rows)
    ends = jnp.zeros((rows, LANES), jnp.float32)
    for plane in range(planes):
        low, high = HALO * plane, width - HALO + HALO * plane
        mask = ((lane >= low) & (lane < low + HALO)) | ((lane >= high) & (lane < high + HALO))
        own = level.v[slot, HALO + plane, pl.ds(2 * PAD, rows), :]
        ends = jnp.where(mask, pltpu.roll(own, low, 1) if low else own, ends)
    level.ends[turn] = ends

    def part(step, first, count, size):
        if step == 0:
            return (first, count), (first, count)
        if step > 0:
            return (first + count - size, size), (first - size, size)
        return (first, size), (first + count, size)

    copies = []
    for along in (-1, 0, 1):
        (src_x, n_x), (dst_x, _) = part(along, HALO, planes, HALO)
        for across in (-1, 0, 1):
            (src_y, n_y), (dst_y, _) = part(across, PAD, rows, PAD)
            for depth in (-1, 0, 1):
                number = (along + 1) * 9 + (across + 1) * 3 + depth + 1
                if number == 13:
                    continue
                if depth == 0:
                    src = level.v.at[slot, pl.ds(src_x, n_x), pl.ds(PAD + src_y, n_y), :]
                    dst = level.v.at[slot, pl.ds(dst_x, n_x), pl.ds(PAD + dst_y, n_y), :]
                else:
                    src = level.ends.at[turn, pl.ds(src_y - PAD, n_y), :]
                    dst = level.met.at[turn, (1 - depth) // 2, 1 - along, pl.ds(dst_y, n_y), :]
                where = {}
                for axis, step in (("gx", along), ("gy", across), ("gz", depth)):
                    if step:
                        where.update(around(axis, step))
                copy = pltpu.make_async_remote_copy(
                    src_ref=src,
                    dst_ref=dst,
                    send_sem=level.send.at[turn, number],
                    recv_sem=level.recv.at[turn, number],
                    device_id=where,
                    device_id_type=MESH,
                )
                copy.start()
                copies.append(copy)
    return copies


def wide_pull(level, slot, copies):
    planes, width, tall, turn = level.planes, level.width, level.tall, slot - 2
    lane = lanes_of(tall)
    for copy in copies:
        copy.wait()
    halo = (lane >= LANES - HALO) | ((lane >= width) & (lane < width + HALO))
    for side in range(3):
        below, above = level.met[turn, 0, side], level.met[turn, 1, side]
        if width < LANES // 2:
            below = pltpu.roll(below, LANES - 2 * width, 1)
        both = jnp.where(lane < HALO * planes, above, below)
        first, count, place = (
            (planes - HALO, HALO, 0),
            (0, planes, HALO),
            (0, HALO, HALO + planes),
        )[side]
        for k in range(count):
            shift = (width - HALO * (first + k)) % LANES
            moved = pltpu.roll(both, shift, 1) if shift else both
            old = level.v[slot, place + k, pl.ds(PAD, tall), :]
            level.v[slot, place + k, pl.ds(PAD, tall), :] = jnp.where(halo, moved, old)


def wide_neighbours(level, slot, plane, first, rows):
    at = lambda p, r: level.v[slot, p, pl.ds(r, rows), :]
    center = at(plane, first)
    return center, (
        at(plane - 1, first),
        at(plane + 1, first),
        at(plane, first - 1),
        at(plane, first + 1),
        pltpu.roll(center, 1, 1),
        pltpu.roll(center, LANES - 1, 1),
    )


def wide_change(level, slot, plane, first, rows):
    center, values = wide_neighbours(level, slot, plane, first, rows)
    total = level.v[RHS, plane, pl.ds(first, rows), :] - WEIGHT * center
    for number, value in enumerate(values):
        total = total + level.off[number, plane, pl.ds(first - PAD, rows), :] * value
    return center, total


def wide_sweep(level, slot, into, layers):
    for plane in range(HALO - layers, HALO + level.planes + layers):
        center, total = wide_change(level, slot, plane, PAD, level.tall)
        level.v[into, plane, pl.ds(PAD, level.tall), :] = center + total


def wide_residual(level, slot):
    for plane in range(level.planes):
        at = pl.ds(plane * level.rows, level.rows)
        total = wide_change(level, slot, HALO + plane, 2 * PAD, level.rows)[1]
        level.res[at, :] = total * level.diag[at, :]


def wide_put(level, slot, values):
    for plane in range(level.planes):
        level.v[slot, HALO + plane, pl.ds(2 * PAD, level.rows), :] = values[
            plane * level.rows : (plane + 1) * level.rows, :
        ]


def wide_prolong(level, slot, into, coarse):
    spread(level, coarse)
    size = level.rows // 2
    for plane in range(level.planes):
        parent = level.half[pl.ds((plane // 2) * size, size), :]
        for q in range(2):
            at = pl.ds(2 * PAD + q, size, stride=2)
            level.v[into, HALO + plane, at, :] = level.v[slot, HALO + plane, at, :] + parent


def wide_own(level, slot):
    inside = lanes_of(level.rows) < level.width
    own = [
        jnp.where(inside, level.v[slot, HALO + plane, pl.ds(2 * PAD, level.rows), :], 0.0)
        for plane in range(level.planes)
    ]
    return jnp.concatenate(own, axis=0)


def wide_coefficients(level, ends):
    rows, tall, planes, width = level.rows, level.tall, level.planes, level.width
    lane = lanes_of(tall)
    row = lax.broadcasted_iota(jnp.int32, (tall, LANES), 0)
    never = row < 0
    known = (lane < width + HALO) | (lane >= LANES - HALO)
    inside = lanes_of(rows) < width
    for plane in range(1, planes + 2 * HALO - 1):
        center, values = wide_neighbours(level, COEF, plane, PAD, tall)
        outside = (
            ends["gx"][0] if plane == HALO else never,
            ends["gx"][1] if plane == HALO + planes - 1 else never,
            (row == PAD) & ends["gy"][0],
            (row == PAD + rows - 1) & ends["gy"][1],
            (lane == 0) & ends["gz"][0],
            (lane == width - 1) & ends["gz"][1],
        )
        faces = [
            0.5 * (center + jnp.where(out, 0.0, value))
            for out, value in zip(outside, values, strict=True)
        ]
        diagonal = sum(faces[1:], faces[0])
        inverse = jnp.where(known, WEIGHT / diagonal, 0.0)
        for number in range(6):
            level.off[number, plane] = jnp.where(outside[number], 0.0, faces[number] * inverse)
        if HALO <= plane < HALO + planes:
            at = pl.ds((plane - HALO) * rows, rows)
            own = slice(PAD, PAD + rows)
            level.inverse[at, :] = jnp.where(inside, inverse[own] * (1.0 / level.scale), 0.0)
            level.diag[at, :] = jnp.where(inside, diagonal[own] * (level.scale / WEIGHT), 0.0)


def gather_ring(field, which, co, place, around):
    rows = field.shape[0] // 2
    tile = pltpu.roll(field[:rows, :], place["lane"], 1) + pltpu.roll(
        field[rows:, :], place["lane"] + LANES // 2, 1
    )
    co["tile"][pl.ds(which * 8, 8), :] = tile
    copies = []
    for step in range(1, place["count"]["gz"]):
        copy = pltpu.make_async_remote_copy(
            src_ref=co["tile"].at[pl.ds(which * 8, 8), :],
            dst_ref=co["tiles"].at[pl.ds((which * 4 + step) * 8, 8), :],
            send_sem=co["ring_send"].at[which, step],
            recv_sem=co["ring_recv"].at[which, step],
            device_id=around("gz", step),
            device_id_type=MESH,
        )
        copy.start()
        copies.append(copy)
    return tile, copies


def gather_plane(tile, copies, which, co, place, around):
    for copy in copies:
        copy.wait()
    for step in range(1, place["count"]["gz"]):
        tile = tile + co["tiles"][pl.ds((which * 4 + step) * 8, 8), :]
    mine = co["whole"].at[which, pl.ds(place["row"], 8), :]
    mine[...] = tile
    for along in range(place["count"]["gx"]):
        for across in range(place["count"]["gy"]):
            if along == 0 and across == 0:
                continue
            pltpu.make_async_remote_copy(
                src_ref=mine,
                dst_ref=mine,
                send_sem=co["plane_send"].at[which],
                recv_sem=co["plane_recv"].at[which],
                device_id={**around("gx", along), **around("gy", across)},
                device_id_type=MESH,
            ).start()


def gather_wait(which, co):
    total = co["whole"].shape[1]
    others = co["whole"].at[which, pl.ds(0, total - 8), :]
    pltpu.make_async_copy(others, others, co["plane_send"].at[which]).wait()
    pltpu.make_async_copy(others, others, co["plane_recv"].at[which]).wait()


def coarse_solve(co, scale):
    total = co["whole"].shape[1]
    count, rows = co["whole"].shape[1] // 32, 32
    lane = lanes_of(rows)
    row = lax.broadcasted_iota(jnp.int32, (rows, LANES), 0)
    low = lane < LANES // 2
    depth = lane & (LANES // 2 - 1)

    def around_of(read, group):
        center = read(group)
        swap = lambda g: pltpu.roll(read(g), LANES // 2, 1)
        here = swap(group)
        before = swap(group - 1) if group > 0 else here
        after = swap(group + 1) if group < count - 1 else here
        return center, (
            jnp.where(low, before, here),
            jnp.where(low, here, after),
            pltpu.roll(center, 1, 0),
            pltpu.roll(center, rows - 1, 0),
            pltpu.roll(center, 1, 1),
            pltpu.roll(center, LANES - 1, 1),
        )

    read_coef = lambda g: co["whole"][0, pl.ds(g * rows, rows), :]
    for group in range(count):
        center, values = around_of(read_coef, group)
        never = row < 0
        outside = (
            low if group == 0 else never,
            ~low if group == count - 1 else never,
            row == 0,
            row == rows - 1,
            depth == 0,
            depth == LANES // 2 - 1,
        )
        faces = [
            0.5 * (center + jnp.where(out, 0.0, value))
            for out, value in zip(outside, values, strict=True)
        ]
        diagonal = sum(faces[1:], faces[0])
        inverse = WEIGHT / diagonal
        at = pl.ds(group * rows, rows)
        for number in range(6):
            co["off"][number, at, :] = jnp.where(outside[number], 0.0, faces[number] * inverse)
        co["inverse"][at, :] = inverse * (1.0 / scale)

    yield

    start = co["whole"][1] * co["inverse"][...]
    co["inverse"][...] = start
    co["v"][0] = jnp.zeros((total, LANES), jnp.float32)

    def one(slot):
        read = lambda g: co["v"][slot, pl.ds(g * rows, rows), :]
        for group in range(count):
            center, values = around_of(read, group)
            at = pl.ds(group * rows, rows)
            new = co["inverse"][at, :] + (1.0 - WEIGHT) * center
            for number, value in enumerate(values):
                new = new + co["off"][number, at, :] * value
            co["v"][1 - slot, at, :] = new

    def pair(_, carry):
        one(0)
        one(1)
        return carry

    lax.fori_loop(0, COARSE // 2, pair, 0)


def kernel(shapes, counts, table, source, guess, classes, out_u, out_r, refs, co):
    top = Level(0, shapes[0], refs[0])
    lower = [Wide(index, shapes[index], refs[index]) for index in range(1, len(shapes))]
    position = {axis: lax.axis_index(axis) for axis in counts}

    def around(axis, step):
        count = counts[axis]
        return {axis: lax.rem(position[axis] + (step + count), count)}

    ends = {axis: (position[axis] == 0, position[axis] == counts[axis] - 1) for axis in counts}
    piece = shapes[-1][2] // 2
    place = dict(
        count=counts,
        lane=position["gz"] * piece,
        row=pl.multiple_of(position["gx"] * 32 + position["gy"] * 8, 8),
    )

    partners = set()
    for along in range(counts["gx"]):
        for across in range(counts["gy"]):
            partners.add((along, across, 0))
    for depth in range(counts["gz"]):
        partners.add((0, 0, depth))
    for along in (-1, 0, 1):
        for across in (-1, 0, 1):
            for depth in (-1, 0, 1):
                partners.add((along % counts["gx"], across % counts["gy"], depth % counts["gz"]))
    partners = sorted(partners - {(0, 0, 0)})
    barrier = pltpu.get_barrier_semaphore()
    for along, across, depth in partners:
        where = {**around("gx", along), **around("gy", across), **around("gz", depth)}
        pl.semaphore_signal(barrier, inc=1, device_id=where, device_id_type=MESH)

    entries = [table[k] for k in range(8)]
    held_c = held_v = jnp.zeros((top.rows, LANES), jnp.float32)
    for plane in range(top.planes):
        at = pl.ds(plane * top.rows, top.rows)
        kind = classes[at, :]
        pick = entries
        for k in range(3):
            bit = (kind & (1 << k)) != 0
            pick = [jnp.where(bit, pick[2 * m + 1], pick[2 * m]) for m in range(len(pick) // 2)]
        values = guess[at, :]
        top.v[pl.ds(top.row(2, 1) + plane * top.pitch, top.rows), :] = pick[0]
        top.v[pl.ds(top.row(0, 1) + plane * top.pitch, top.rows), :] = values
        held_c = pack(top, plane, pick[0], held_c)
        held_v = pack(top, plane, values, held_v)
    pl.semaphore_wait(barrier, len(partners))

    moving = push(top, 2, held_c, around)
    first = push(top, 0, held_v, around)
    coarse = restrict(
        top, lambda plane, q, n: top.v[pl.ds(top.row(2, 1) + plane * top.pitch + q, n, stride=2), :]
    )
    wide_moving = []
    for level in lower:
        wide_put(level, COEF, coarse)
        wide_moving.append(wide_push(level, COEF, around))
        coarse = restrict(
            level,
            lambda plane, q, n: level.v[COEF, HALO + plane, pl.ds(2 * PAD + q, n, stride=2), :],
        )
    tile, copies = gather_ring(coarse, 0, co, place, around)
    pull(top, 2, moving)
    coefficients(top, ends)
    top.rhs[...] = source[...] * top.inverse[...]
    pull(top, 0, first)
    held = sweep(top, 0)

    def ready(level, copies):
        wide_pull(level, COEF, copies)
        wide_coefficients(level, ends)

    solve = coarse_solve(co, 0.25**LEVELS)

    def ready_coarse():
        gather_wait(0, co)
        next(solve)

    between = [functools.partial(gather_plane, tile, copies, 0, co, place, around)]
    between += [functools.partial(ready, *pair) for pair in zip(lower, wide_moving, strict=True)]
    slot, held = smooth(top, 1, held, around, SWEEPS - 1, between)
    copies = push(top, slot, held, around)
    ready_coarse()
    pull(top, slot, copies)
    residual(top, slot, top.res)
    fine = slot
    rhs = restrict(top, lambda plane, q, n: top.res[pl.ds(plane * top.rows + q, n, stride=2), :])
    for level in lower:
        wide_put(level, RHS, rhs * level.inverse[...])
        wide_pull(level, RHS, wide_push(level, RHS, around))
        slot = RHS
        for count in range(SWEEPS - 1):
            wide_sweep(level, slot, count % 2, HALO - 1 - count)
            slot = count % 2
        wide_residual(level, slot)
        rhs = restrict(
            level, lambda plane, q, n: level.res[pl.ds(plane * level.rows + q, n, stride=2), :]
        )

    tile, copies = gather_ring(rhs, 1, co, place, around)
    gather_plane(tile, copies, 1, co, place, around)
    gather_wait(1, co)
    next(solve, None)

    mine = co["v"][0, pl.ds(place["row"], 8), :]
    inside = lanes_of(8) < piece
    back = LANES - place["lane"]
    coarse = jnp.concatenate(
        [
            jnp.where(inside, pltpu.roll(mine, back & (LANES - 1), 1), 0.0),
            jnp.where(inside, pltpu.roll(mine, (back + LANES // 2) & (LANES - 1), 1), 0.0),
        ],
        axis=0,
    )
    for level in reversed(lower):
        wide_prolong(level, (SWEEPS - 2) % 2, AFTER, coarse)
        wide_pull(level, AFTER, wide_push(level, AFTER, around))
        slot = AFTER
        for count in range(SWEEPS):
            wide_sweep(level, slot, count % 2, HALO - 1 - count)
            slot = count % 2
        coarse = wide_own(level, slot)
    held = prolong(top, fine, coarse)
    slot, held = smooth(top, 1 - fine, held, around, SWEEPS)
    copies = push(top, slot, held, around)
    for plane in range(top.planes):
        out_u[pl.ds(plane * top.rows, top.rows), :] = top.v[pl.ds(top.row(slot, plane + 1), top.rows), :]
    pull(top, slot, copies)
    residual(top, slot, out_r)


def body(counts, source, first_guess, cell_classes, class_table):
    planes, rows, width = source.shape
    shapes = [(planes >> k, rows >> k, width >> k) for k in range(LEVELS)]
    flat = (planes * rows, width)
    whole = counts["gx"] * 32
    f32 = jnp.float32
    co = dict(
        tile=pltpu.VMEM((2 * 8, LANES), f32),
        tiles=pltpu.VMEM((2 * 4 * 8, LANES), f32),
        whole=pltpu.VMEM((2, whole, LANES), f32),
        off=pltpu.VMEM((6, whole, LANES), f32),
        inverse=pltpu.VMEM((whole, LANES), f32),
        v=pltpu.VMEM((2, whole, LANES), f32),
        ring_send=pltpu.SemaphoreType.DMA((2, 4)),
        ring_recv=pltpu.SemaphoreType.DMA((2, 4)),
        plane_send=pltpu.SemaphoreType.DMA((2,)),
        plane_recv=pltpu.SemaphoreType.DMA((2,)),
    )
    vmem = pl.BlockSpec(memory_space=pltpu.VMEM)
    solution_out, residual_out = pl.pallas_call(
        functools.partial(kernel, shapes, counts),
        out_shape=[jax.ShapeDtypeStruct(flat, f32)] * 2,
        in_specs=[pl.BlockSpec(memory_space=pltpu.SMEM), vmem, vmem, vmem],
        out_specs=[vmem, vmem],
        scratch_shapes=[[level_scratch(shapes[0])] + [wide_scratch(shape) for shape in shapes[1:]], co],
        compiler_params=pltpu.CompilerParams(
            collective_id=0, has_side_effects=True, vmem_limit_bytes=48 * 1024 * 1024
        ),
        cost_estimate=pl.CostEstimate(flops=100_000_000, bytes_accessed=3_000_000, transcendentals=0),
        name="vcycle",
    )(class_table, source.reshape(flat), first_guess.reshape(flat), cell_classes.reshape(flat))
    return solution_out.reshape(source.shape), residual_out.reshape(source.shape)


def solution(mesh):
    counts = {axis: mesh.shape[axis] for axis in ("gx", "gy", "gz")}
    spec = P("gx", "gy", "gz")
    return jax.shard_map(
        functools.partial(body, counts),
        mesh=mesh,
        in_specs=(spec, spec, spec, P()),
        out_specs=(spec, spec),
        check_vma=False,
    )
```

```python
import functools

import jax
import jax.numpy as jnp
from jax import lax
from jax.experimental import pallas as pl
from jax.experimental.pallas import tpu as pltpu
from jax.sharding import PartitionSpec as P

LEVELS = 3
SWEEPS = 4
COARSE = 16
WEIGHT = 0.85
LANES = 128
PAD = 8
HALO = 4
MESH = pl.DeviceIdType.MESH
HIGHEST = lax.Precision.HIGHEST


class Level:
    def __init__(self, index, shape, refs):
        self.index = index
        self.planes, self.rows, self.width = shape
        self.pitch = self.rows + 2 * PAD
        self.scale = 0.25**index
        self.packed = max(self.planes, 8)
        for name, ref in refs.items():
            setattr(self, name, ref)

    def row(self, slot, plane):
        return (slot * (self.planes + 2) + plane) * self.pitch + PAD


def level_scratch(shape):
    planes, rows, _ = shape
    f32 = jnp.float32
    packed = max(planes, 8)
    flat = planes * rows
    return dict(
        v=pltpu.VMEM((3 * (planes + 2) * (rows + 2 * PAD), LANES), f32),
        ysend=pltpu.VMEM((3 * 2 * packed, LANES), f32),
        yrecv=pltpu.VMEM((3 * 2 * packed, LANES), f32),
        zsend=pltpu.VMEM((3 * rows, LANES), f32),
        zrecv=pltpu.VMEM((3 * 2 * rows, LANES), f32),
        edge=pltpu.VMEM((rows, LANES), f32),
        yface=pltpu.VMEM((2 * packed, LANES), f32),
        zface=pltpu.VMEM((rows, LANES), f32),
        off=pltpu.VMEM((6 * flat, LANES), f32),
        rhs=pltpu.VMEM((flat, LANES), f32),
        inverse=pltpu.VMEM((flat, LANES), f32),
        diag=pltpu.VMEM((flat, LANES), f32),
        res=pltpu.VMEM((flat, LANES), f32),
        half=pltpu.VMEM((max(flat // 4, 8), LANES), f32),
        send=pltpu.SemaphoreType.DMA((3, 6)),
        recv=pltpu.SemaphoreType.DMA((3, 6)),
    )


def lanes_of(rows):
    return lax.broadcasted_iota(jnp.int32, (rows, LANES), 1)


def pack(level, plane, values, held):
    lane = lanes_of(level.rows)
    first = 2 * plane + 1
    mask = (lane == first) | (lane == ((first + level.width - 1) & (LANES - 1)))
    return jnp.where(mask, pltpu.roll(values, first, 1), held)


def push(level, slot, held, around):
    planes, rows, packed = level.planes, level.rows, level.packed
    level.zsend[pl.ds(slot * rows, rows), :] = held
    for side, row in ((0, 0), (1, rows - 1)):
        level.ysend[pl.ds((slot * 2 + side) * packed, planes), :] = level.v[
            pl.ds(level.row(slot, 1) + row, planes, stride=level.pitch), :
        ]
    own = lambda plane: level.v.at[pl.ds(level.row(slot, plane), rows), :]
    ysend = lambda side: level.ysend.at[pl.ds((slot * 2 + side) * packed, packed), :]
    yrecv = lambda side: level.yrecv.at[pl.ds((slot * 2 + side) * packed, packed), :]
    zsend = level.zsend.at[pl.ds(slot * rows, rows), :]
    zrecv = lambda side: level.zrecv.at[pl.ds((slot * 2 + side) * rows, rows), :]
    plan = (
        (own(planes), own(0), "gx", 1),
        (own(1), own(planes + 1), "gx", -1),
        (ysend(1), yrecv(0), "gy", 1),
        (ysend(0), yrecv(1), "gy", -1),
        (zsend, zrecv(0), "gz", 1),
        (zsend, zrecv(1), "gz", -1),
    )
    copies = []
    for number, (src, dst, axis, step) in enumerate(plan):
        copy = pltpu.make_async_remote_copy(
            src_ref=src,
            dst_ref=dst,
            send_sem=level.send.at[slot, number],
            recv_sem=level.recv.at[slot, number],
            device_id=around(axis, step),
            device_id_type=MESH,
        )
        copy.start()
        copies.append(copy)
    return copies


def pull(level, slot, copies):
    planes, rows, packed, width = level.planes, level.rows, level.packed, level.width
    for copy in copies:
        copy.wait()
    for side, row in ((0, -1), (1, rows)):
        level.v[pl.ds(level.row(slot, 1) + row, planes, stride=level.pitch), :] = level.yrecv[
            pl.ds((slot * 2 + side) * packed, planes), :
        ]
    below = level.zrecv[pl.ds(slot * 2 * rows, rows), :]
    above = level.zrecv[pl.ds((slot * 2 + 1) * rows, rows), :]
    if width < LANES:
        below = pltpu.roll(below, LANES - width, 1)
    above = pltpu.roll(above, width - 2, 1)
    level.edge[...] = jnp.where((lanes_of(rows) & 1) == 0, below, above)


def neighbours(level, slot, plane, center):
    rows, width = level.rows, level.width
    first = level.row(slot, 1) + plane * level.pitch
    at = lambda shift: level.v[pl.ds(first + shift, rows), :]
    lane = lanes_of(rows)
    edge = pltpu.roll(level.edge[...], (LANES - 2 * plane) & (LANES - 1), 1)
    return (
        at(-level.pitch),
        at(level.pitch),
        at(-1),
        at(1),
        jnp.where(lane == 0, edge, pltpu.roll(center, 1, 1)),
        jnp.where(lane == width - 1, edge, pltpu.roll(center, LANES - 1, 1)),
    )


def partial(level, slot, residual):
    rows, planes, flat = level.rows, level.planes, level.planes * level.rows
    for plane in range(planes):
        first = level.row(slot, 1) + plane * level.pitch
        at = lambda shift: level.v[pl.ds(first + shift, rows), :]
        off = lambda number: level.off[pl.ds(number * flat + plane * rows, rows), :]
        center = at(0)
        keep = -WEIGHT if residual else 1.0 - WEIGHT
        total = level.rhs[pl.ds(plane * rows, rows), :] + keep * center
        if plane > 0:
            total = total + off(0) * at(-level.pitch)
        if plane < planes - 1:
            total = total + off(1) * at(level.pitch)
        total = total + off(2) * at(-1) + off(3) * at(1)
        total = total + off(4) * pltpu.roll(center, 1, 1) + off(5) * pltpu.roll(center, LANES - 1, 1)
        if residual:
            level.res[pl.ds(plane * rows, rows), :] = total
        else:
            level.v[pl.ds(level.row(1 - slot, 1) + plane * level.pitch, rows), :] = total


def complete(level, slot, copies, out=None):
    planes, rows, packed, width = level.planes, level.rows, level.packed, level.width
    flat = planes * rows
    for copy in copies:
        copy.wait()
    ref, base, pitch = (level.v, level.row(1 - slot, 1), level.pitch) if out is None else (level.res, 0, rows)
    for number, plane, there in ((0, 0, 0), (1, planes - 1, planes + 1)):
        at = pl.ds(base + plane * pitch, rows)
        ref[at, :] = ref[at, :] + (
            level.off[pl.ds(number * flat + plane * rows, rows), :]
            * level.v[pl.ds(level.row(slot, there), rows), :]
        )
    for side, row in ((0, 0), (1, rows - 1)):
        at = pl.ds(base + row, planes, stride=pitch)
        ref[at, :] = ref[at, :] + (
            level.yface[pl.ds(side * packed, planes), :]
            * level.yrecv[pl.ds((slot * 2 + side) * packed, planes), :]
        )
    below = level.zrecv[pl.ds(slot * 2 * rows, rows), :]
    above = pltpu.roll(level.zrecv[pl.ds((slot * 2 + 1) * rows, rows), :], width - 2, 1)
    lane = lanes_of(rows)
    edge = jnp.where((lane & 1) == 0, below, above) * level.zface[...]
    ends = (lane == 0) | (lane == width - 1)
    held = jnp.zeros((rows, LANES), jnp.float32)
    for plane in range(planes):
        at = pl.ds(base + plane * pitch, rows)
        shift = (LANES - 2 * plane) & (LANES - 1)
        moved = pltpu.roll(edge, shift, 1) if shift else edge
        new = ref[at, :] + jnp.where(ends, moved, 0.0)
        if out is None:
            ref[at, :] = new
            held = pack(level, plane, new, held)
        else:
            here = pl.ds(plane * rows, rows)
            out[here, :] = new * level.diag[here, :]
    return held


def smooth(level, slot, held, around, count, between=()):
    between = list(between)
    for _ in range(count):
        copies = push(level, slot, held, around)
        partial(level, slot, False)
        if between:
            between.pop(0)()
        held = complete(level, slot, copies)
        slot = 1 - slot
    return slot, held


def restrict(level, read):
    size = level.rows // 2
    for plane in range(level.planes // 2):
        parts = [read(2 * plane + p, q, size) for p in range(2) for q in range(2)]
        level.half[pl.ds(plane * size, size), :] = (parts[0] + parts[1]) + (parts[2] + parts[3])
    row = lax.broadcasted_iota(jnp.int32, (LANES, LANES), 0)
    column = lax.broadcasted_iota(jnp.int32, (LANES, LANES), 1)
    gather = jnp.where((row >> 1) == column, 0.125, 0.0)
    return lax.dot(level.half[...], gather, precision=HIGHEST, preferred_element_type=jnp.float32)


def spread(level, coarse):
    row = lax.broadcasted_iota(jnp.int32, (LANES, LANES), 0)
    column = lax.broadcasted_iota(jnp.int32, (LANES, LANES), 1)
    twice = jnp.where(row == (column >> 1), 1.0, 0.0)
    level.half[...] = lax.dot(coarse, twice, precision=HIGHEST, preferred_element_type=jnp.float32)


def prolong(level, slot, coarse):
    spread(level, coarse)
    size = level.rows // 2
    held = jnp.zeros((level.rows, LANES), jnp.float32)
    for plane in range(level.planes):
        parent = level.half[pl.ds((plane // 2) * size, size), :]
        old, new = level.row(slot, plane + 1), level.row(1 - slot, plane + 1)
        for q in range(2):
            level.v[pl.ds(new + q, size, stride=2), :] = (
                level.v[pl.ds(old + q, size, stride=2), :] + parent
            )
        held = pack(level, plane, level.v[pl.ds(new, level.rows), :], held)
    return held


def coefficients(level, ends):
    rows, planes, width, flat = level.rows, level.planes, level.width, level.planes * level.rows
    lane = lanes_of(rows)
    row = lax.broadcasted_iota(jnp.int32, (rows, LANES), 0)

    never = row < 0
    zface = jnp.zeros((rows, LANES), jnp.float32)
    for plane in range(planes):
        center = level.v[pl.ds(level.row(2, 1) + plane * level.pitch, rows), :]
        outside = (
            ends["gx"][0] if plane == 0 else never,
            ends["gx"][1] if plane == planes - 1 else never,
            (row == 0) & ends["gy"][0],
            (row == rows - 1) & ends["gy"][1],
            (lane == 0) & ends["gz"][0],
            (lane == width - 1) & ends["gz"][1],
        )
        faces = [
            0.5 * (center + jnp.where(out, 0.0, value))
            for out, value in zip(outside, neighbours(level, 2, plane, center), strict=True)
        ]
        diagonal = sum(faces[1:], faces[0])
        inverse = WEIGHT / diagonal
        at = pl.ds(plane * rows, rows)
        level.inverse[at, :] = inverse
        level.diag[at, :] = diagonal * (1.0 / WEIGHT)
        off = [jnp.where(out, 0.0, face * inverse) for out, face in zip(outside, faces, strict=True)]
        level.yface[pl.ds(plane, 1), :] = off[2][:1]
        level.yface[pl.ds(level.packed + plane, 1), :] = off[3][rows - 1 :]
        low = pltpu.roll(off[4], 2 * plane, 1) if plane else off[4]
        high = pltpu.roll(off[5], 2 * plane, 1) if plane else off[5]
        zface = jnp.where(lane == 2 * plane, low, zface)
        zface = jnp.where(lane == ((2 * plane - 1) & (LANES - 1)), high, zface)
        border = (never, never, row == 0, row == rows - 1, lane == 0, lane == width - 1)
        for number in range(6):
            value = off[number] if number < 2 else jnp.where(border[number], 0.0, off[number])
            level.off[pl.ds(number * flat + plane * rows, rows), :] = value
    level.zface[...] = zface


class Wide:
    def __init__(self, index, shape, refs):
        self.index = index
        self.planes, self.rows, self.width = shape
        self.tall = self.rows + 2 * PAD
        self.scale = 0.25**index
        for name, ref in refs.items():
            setattr(self, name, ref)


COEF, RHS, AFTER = 2, 3, 4


def wide_scratch(shape):
    planes, rows, _ = shape
    f32 = jnp.float32
    deep, tall = planes + 2 * HALO, rows + 2 * PAD
    return dict(
        v=pltpu.VMEM((5, deep, tall + 2 * PAD, LANES), f32),
        ends=pltpu.VMEM((3, rows, LANES), f32),
        met=pltpu.VMEM((3, 2, 3, tall, LANES), f32),
        off=pltpu.VMEM((6, deep, tall, LANES), f32),
        inverse=pltpu.VMEM((planes * rows, LANES), f32),
        diag=pltpu.VMEM((planes * rows, LANES), f32),
        res=pltpu.VMEM((planes * rows, LANES), f32),
        half=pltpu.VMEM((planes * rows // 4, LANES), f32),
        send=pltpu.SemaphoreType.DMA((3, 27)),
        recv=pltpu.SemaphoreType.DMA((3, 27)),
    )


def wide_push(level, slot, around):
    planes, rows, width, turn = level.planes, level.rows, level.width, slot - 2
    lane = lanes_of(rows)
    ends = jnp.zeros((rows, LANES), jnp.float32)
    for plane in range(planes):
        low, high = HALO * plane, width - HALO + HALO * plane
        mask = ((lane >= low) & (lane < low + HALO)) | ((lane >= high) & (lane < high + HALO))
        own = level.v[slot, HALO + plane, pl.ds(2 * PAD, rows), :]
        ends = jnp.where(mask, pltpu.roll(own, low, 1) if low else own, ends)
    level.ends[turn] = ends

    def part(step, first, count, size):
        if step == 0:
            return (first, count), (first, count)
        if step > 0:
            return (first + count - size, size), (first - size, size)
        return (first, size), (first + count, size)

    copies = []
    steps = [(a, b, c) for a in (-1, 0, 1) for b in (-1, 0, 1) for c in (-1, 0, 1)]
    for along, across, depth in sorted(steps, key=lambda d: -sum(abs(k) for k in d)):
        (src_x, n_x), (dst_x, _) = part(along, HALO, planes, HALO)
        (src_y, n_y), (dst_y, _) = part(across, PAD, rows, PAD)
        number = (along + 1) * 9 + (across + 1) * 3 + depth + 1
        if number == 13:
            continue
        if depth == 0:
            src = level.v.at[slot, pl.ds(src_x, n_x), pl.ds(PAD + src_y, n_y), :]
            dst = level.v.at[slot, pl.ds(dst_x, n_x), pl.ds(PAD + dst_y, n_y), :]
        else:
            src = level.ends.at[turn, pl.ds(src_y - PAD, n_y), :]
            dst = level.met.at[turn, (1 - depth) // 2, 1 - along, pl.ds(dst_y, n_y), :]
        where = {}
        for axis, step in (("gx", along), ("gy", across), ("gz", depth)):
            if step:
                where.update(around(axis, step))
        copy = pltpu.make_async_remote_copy(
            src_ref=src,
            dst_ref=dst,
            send_sem=level.send.at[turn, number],
            recv_sem=level.recv.at[turn, number],
            device_id=where,
            device_id_type=MESH,
        )
        copy.start()
        copies.append(copy)
    return copies


def wide_pull(level, slot, copies):
    planes, width, tall, turn = level.planes, level.width, level.tall, slot - 2
    lane = lanes_of(tall)
    for copy in copies:
        copy.wait()
    halo = (lane >= LANES - HALO) | ((lane >= width) & (lane < width + HALO))
    for side in range(3):
        below, above = level.met[turn, 0, side], level.met[turn, 1, side]
        if width < LANES // 2:
            below = pltpu.roll(below, LANES - 2 * width, 1)
        both = jnp.where(lane < HALO * planes, above, below)
        first, count, place = (
            (planes - HALO, HALO, 0),
            (0, planes, HALO),
            (0, HALO, HALO + planes),
        )[side]
        for k in range(count):
            shift = (width - HALO * (first + k)) % LANES
            moved = pltpu.roll(both, shift, 1) if shift else both
            old = level.v[slot, place + k, pl.ds(PAD, tall), :]
            level.v[slot, place + k, pl.ds(PAD, tall), :] = jnp.where(halo, moved, old)


def wide_neighbours(level, slot, plane, first, rows):
    at = lambda p, r: level.v[slot, p, pl.ds(r, rows), :]
    center = at(plane, first)
    return center, (
        at(plane - 1, first),
        at(plane + 1, first),
        at(plane, first - 1),
        at(plane, first + 1),
        pltpu.roll(center, 1, 1),
        pltpu.roll(center, LANES - 1, 1),
    )


def wide_change(level, slot, plane, first, rows):
    center, values = wide_neighbours(level, slot, plane, first, rows)
    total = level.v[RHS, plane, pl.ds(first, rows), :] - WEIGHT * center
    for number, value in enumerate(values):
        total = total + level.off[number, plane, pl.ds(first - PAD, rows), :] * value
    return center, total


def wide_sweep(level, slot, into, layers):
    for plane in range(HALO - layers, HALO + level.planes + layers):
        center, total = wide_change(level, slot, plane, PAD, level.tall)
        level.v[into, plane, pl.ds(PAD, level.tall), :] = center + total


def wide_residual(level, slot):
    for plane in range(level.planes):
        at = pl.ds(plane * level.rows, level.rows)
        total = wide_change(level, slot, HALO + plane, 2 * PAD, level.rows)[1]
        level.res[at, :] = total * level.diag[at, :]


def wide_put(level, slot, values):
    for plane in range(level.planes):
        level.v[slot, HALO + plane, pl.ds(2 * PAD, level.rows), :] = values[
            plane * level.rows : (plane + 1) * level.rows, :
        ]


def wide_prolong(level, slot, into, coarse):
    spread(level, coarse)
    size = level.rows // 2
    for plane in range(level.planes):
        parent = level.half[pl.ds((plane // 2) * size, size), :]
        for q in range(2):
            at = pl.ds(2 * PAD + q, size, stride=2)
            level.v[into, HALO + plane, at, :] = level.v[slot, HALO + plane, at, :] + parent


def wide_own(level, slot):
    inside = lanes_of(level.rows) < level.width
    own = [
        jnp.where(inside, level.v[slot, HALO + plane, pl.ds(2 * PAD, level.rows), :], 0.0)
        for plane in range(level.planes)
    ]
    return jnp.concatenate(own, axis=0)


def wide_coefficients(level, ends):
    rows, tall, planes, width = level.rows, level.tall, level.planes, level.width
    lane = lanes_of(tall)
    row = lax.broadcasted_iota(jnp.int32, (tall, LANES), 0)
    never = row < 0
    known = (lane < width + HALO) | (lane >= LANES - HALO)
    inside = lanes_of(rows) < width
    for plane in range(1, planes + 2 * HALO - 1):
        center, values = wide_neighbours(level, COEF, plane, PAD, tall)
        outside = (
            ends["gx"][0] if plane == HALO else never,
            ends["gx"][1] if plane == HALO + planes - 1 else never,
            (row == PAD) & ends["gy"][0],
            (row == PAD + rows - 1) & ends["gy"][1],
            (lane == 0) & ends["gz"][0],
            (lane == width - 1) & ends["gz"][1],
        )
        faces = [
            0.5 * (center + jnp.where(out, 0.0, value))
            for out, value in zip(outside, values, strict=True)
        ]
        diagonal = sum(faces[1:], faces[0])
        inverse = jnp.where(known, WEIGHT / diagonal, 0.0)
        for number in range(6):
            level.off[number, plane] = jnp.where(outside[number], 0.0, faces[number] * inverse)
        if HALO <= plane < HALO + planes:
            at = pl.ds((plane - HALO) * rows, rows)
            own = slice(PAD, PAD + rows)
            level.inverse[at, :] = jnp.where(inside, inverse[own] * (1.0 / level.scale), 0.0)
            level.diag[at, :] = jnp.where(inside, diagonal[own] * (level.scale / WEIGHT), 0.0)


def gather_ring(field, which, co, place, around):
    rows = field.shape[0] // 2
    tile = pltpu.roll(field[:rows, :], place["lane"], 1) + pltpu.roll(
        field[rows:, :], place["lane"] + LANES // 2, 1
    )
    co["tile"][pl.ds(which * 8, 8), :] = tile
    copies = []
    for step in range(1, place["count"]["gz"]):
        copy = pltpu.make_async_remote_copy(
            src_ref=co["tile"].at[pl.ds(which * 8, 8), :],
            dst_ref=co["tiles"].at[pl.ds((which * 4 + step) * 8, 8), :],
            send_sem=co["ring_send"].at[which, step],
            recv_sem=co["ring_recv"].at[which, step],
            device_id=around("gz", step),
            device_id_type=MESH,
        )
        copy.start()
        copies.append(copy)
    return tile, copies


def gather_plane(tile, copies, which, co, place, around):
    for copy in copies:
        copy.wait()
    for step in range(1, place["count"]["gz"]):
        tile = tile + co["tiles"][pl.ds((which * 4 + step) * 8, 8), :]
    mine = co["whole"].at[which, pl.ds(place["row"], 8), :]
    mine[...] = tile
    for along in range(place["count"]["gx"]):
        for across in range(place["count"]["gy"]):
            if along == 0 and across == 0:
                continue
            pltpu.make_async_remote_copy(
                src_ref=mine,
                dst_ref=mine,
                send_sem=co["plane_send"].at[which],
                recv_sem=co["plane_recv"].at[which],
                device_id={**around("gx", along), **around("gy", across)},
                device_id_type=MESH,
            ).start()


def gather_wait(which, co):
    total = co["whole"].shape[1]
    others = co["whole"].at[which, pl.ds(0, total - 8), :]
    pltpu.make_async_copy(others, others, co["plane_send"].at[which]).wait()
    pltpu.make_async_copy(others, others, co["plane_recv"].at[which]).wait()


def coarse_solve(co, scale):
    total = co["whole"].shape[1]
    count, rows = co["whole"].shape[1] // 32, 32
    lane = lanes_of(rows)
    row = lax.broadcasted_iota(jnp.int32, (rows, LANES), 0)
    low = lane < LANES // 2
    depth = lane & (LANES // 2 - 1)

    def around_of(read, group):
        center = read(group)
        swap = lambda g: pltpu.roll(read(g), LANES // 2, 1)
        here = swap(group)
        before = swap(group - 1) if group > 0 else here
        after = swap(group + 1) if group < count - 1 else here
        return center, (
            jnp.where(low, before, here),
            jnp.where(low, here, after),
            pltpu.roll(center, 1, 0),
            pltpu.roll(center, rows - 1, 0),
            pltpu.roll(center, 1, 1),
            pltpu.roll(center, LANES - 1, 1),
        )

    read_coef = lambda g: co["whole"][0, pl.ds(g * rows, rows), :]
    for group in range(count):
        center, values = around_of(read_coef, group)
        never = row < 0
        outside = (
            low if group == 0 else never,
            ~low if group == count - 1 else never,
            row == 0,
            row == rows - 1,
            depth == 0,
            depth == LANES // 2 - 1,
        )
        faces = [
            0.5 * (center + jnp.where(out, 0.0, value))
            for out, value in zip(outside, values, strict=True)
        ]
        diagonal = sum(faces[1:], faces[0])
        inverse = WEIGHT / diagonal
        at = pl.ds(group * rows, rows)
        for number in range(6):
            co["off"][number, at, :] = jnp.where(outside[number], 0.0, faces[number] * inverse)
        co["inverse"][at, :] = inverse * (1.0 / scale)

    yield

    start = co["whole"][1] * co["inverse"][...]
    co["inverse"][...] = start
    co["v"][0] = jnp.zeros((total, LANES), jnp.float32)

    def one(slot):
        read = lambda g: co["v"][slot, pl.ds(g * rows, rows), :]
        for group in range(count):
            center, values = around_of(read, group)
            at = pl.ds(group * rows, rows)
            new = co["inverse"][at, :] + (1.0 - WEIGHT) * center
            for number, value in enumerate(values):
                new = new + co["off"][number, at, :] * value
            co["v"][1 - slot, at, :] = new

    def pair(_, carry):
        one(0)
        one(1)
        return carry

    lax.fori_loop(0, COARSE // 2, pair, 0)


def kernel(shapes, counts, table_in, source_in, guess_in, classes_in, out_u, out_r, refs, co, got):
    table, source, guess, classes = got["table"], got["source"], got["guess"], got["classes"]
    arriving = [
        pltpu.make_async_copy(src, dst, got["sem"].at[number])
        for number, (src, dst) in enumerate(
            ((table_in, table), (classes_in, classes), (guess_in, guess), (source_in, source))
        )
    ]
    for copy in arriving:
        copy.start()
    top = Level(0, shapes[0], refs[0])
    lower = [Wide(index, shapes[index], refs[index]) for index in range(1, len(shapes))]
    position = {axis: lax.axis_index(axis) for axis in counts}

    def around(axis, step):
        count = counts[axis]
        return {axis: lax.rem(position[axis] + (step + count), count)}

    ends = {axis: (position[axis] == 0, position[axis] == counts[axis] - 1) for axis in counts}
    piece = shapes[-1][2] // 2
    place = dict(
        count=counts,
        lane=position["gz"] * piece,
        row=pl.multiple_of(position["gx"] * 32 + position["gy"] * 8, 8),
    )

    partners = set()
    for along in range(counts["gx"]):
        for across in range(counts["gy"]):
            partners.add((along, across, 0))
    for depth in range(counts["gz"]):
        partners.add((0, 0, depth))
    for along in (-1, 0, 1):
        for across in (-1, 0, 1):
            for depth in (-1, 0, 1):
                partners.add((along % counts["gx"], across % counts["gy"], depth % counts["gz"]))
    partners = sorted(partners - {(0, 0, 0)})
    barrier = pltpu.get_barrier_semaphore()
    for along, across, depth in partners:
        where = {**around("gx", along), **around("gy", across), **around("gz", depth)}
        pl.semaphore_signal(barrier, inc=1, device_id=where, device_id_type=MESH)

    for row in (top.row(0, 1) - 1, top.row(0, 1) + top.rows, top.row(1, 1) - 1, top.row(1, 1) + top.rows):
        top.v[pl.ds(row, top.planes, stride=top.pitch), :] = jnp.zeros((top.planes, LANES), jnp.float32)
    for copy in arriving[:3]:
        copy.wait()
    entries = [table[k] for k in range(8)]
    held_c = held_v = jnp.zeros((top.rows, LANES), jnp.float32)
    for plane in range(top.planes):
        at = pl.ds(plane * top.rows, top.rows)
        kind = classes[at, :]
        pick = entries
        for k in range(3):
            bit = (kind & (1 << k)) != 0
            pick = [jnp.where(bit, pick[2 * m + 1], pick[2 * m]) for m in range(len(pick) // 2)]
        values = guess[at, :]
        top.v[pl.ds(top.row(2, 1) + plane * top.pitch, top.rows), :] = pick[0]
        top.v[pl.ds(top.row(0, 1) + plane * top.pitch, top.rows), :] = values
        held_c = pack(top, plane, pick[0], held_c)
        held_v = pack(top, plane, values, held_v)
    pl.semaphore_wait(barrier, len(partners))

    moving = push(top, 2, held_c, around)
    first = push(top, 0, held_v, around)
    coarse = restrict(
        top, lambda plane, q, n: top.v[pl.ds(top.row(2, 1) + plane * top.pitch + q, n, stride=2), :]
    )
    wide_moving = []
    for level in lower:
        wide_put(level, COEF, coarse)
        wide_moving.append(wide_push(level, COEF, around))
        coarse = restrict(
            level,
            lambda plane, q, n: level.v[COEF, HALO + plane, pl.ds(2 * PAD + q, n, stride=2), :],
        )
    tile, copies = gather_ring(coarse, 0, co, place, around)
    pull(top, 2, moving)
    coefficients(top, ends)
    arriving[3].wait()
    top.rhs[...] = source[...] * top.inverse[...]
    partial(top, 0, False)
    held = complete(top, 0, first)

    def ready(level, copies):
        wide_pull(level, COEF, copies)
        wide_coefficients(level, ends)

    solve = coarse_solve(co, 0.25**LEVELS)

    def ready_coarse():
        gather_wait(0, co)
        next(solve)

    between = [functools.partial(gather_plane, tile, copies, 0, co, place, around)]
    between += [functools.partial(ready, *pair) for pair in zip(lower, wide_moving, strict=True)]
    slot, held = smooth(top, 1, held, around, SWEEPS - 1, between)
    copies = push(top, slot, held, around)
    partial(top, slot, True)
    ready_coarse()
    complete(top, slot, copies, top.res)
    fine = slot
    rhs = restrict(top, lambda plane, q, n: top.res[pl.ds(plane * top.rows + q, n, stride=2), :])
    for level in lower:
        wide_put(level, RHS, rhs * level.inverse[...])
        wide_pull(level, RHS, wide_push(level, RHS, around))
        slot = RHS
        for count in range(SWEEPS - 1):
            wide_sweep(level, slot, count % 2, HALO - 1 - count)
            slot = count % 2
        wide_residual(level, slot)
        rhs = restrict(
            level, lambda plane, q, n: level.res[pl.ds(plane * level.rows + q, n, stride=2), :]
        )

    tile, copies = gather_ring(rhs, 1, co, place, around)
    gather_plane(tile, copies, 1, co, place, around)
    gather_wait(1, co)
    next(solve, None)

    mine = co["v"][0, pl.ds(place["row"], 8), :]
    inside = lanes_of(8) < piece
    back = LANES - place["lane"]
    coarse = jnp.concatenate(
        [
            jnp.where(inside, pltpu.roll(mine, back & (LANES - 1), 1), 0.0),
            jnp.where(inside, pltpu.roll(mine, (back + LANES // 2) & (LANES - 1), 1), 0.0),
        ],
        axis=0,
    )
    for level in reversed(lower):
        wide_prolong(level, (SWEEPS - 2) % 2, AFTER, coarse)
        wide_pull(level, AFTER, wide_push(level, AFTER, around))
        slot = AFTER
        for count in range(SWEEPS):
            wide_sweep(level, slot, count % 2, HALO - 1 - count)
            slot = count % 2
        coarse = wide_own(level, slot)
    held = prolong(top, fine, coarse)
    slot, held = smooth(top, 1 - fine, held, around, SWEEPS)
    copies = push(top, slot, held, around)
    for plane in range(top.planes):
        out_u[pl.ds(plane * top.rows, top.rows), :] = top.v[pl.ds(top.row(slot, plane + 1), top.rows), :]
    partial(top, slot, True)
    complete(top, slot, copies, out_r)


def body(counts, source, first_guess, cell_classes, class_table):
    planes, rows, width = source.shape
    shapes = [(planes >> k, rows >> k, width >> k) for k in range(LEVELS)]
    flat = (planes * rows, width)
    whole = counts["gx"] * 32
    f32 = jnp.float32
    co = dict(
        tile=pltpu.VMEM((2 * 8, LANES), f32),
        tiles=pltpu.VMEM((2 * 4 * 8, LANES), f32),
        whole=pltpu.VMEM((2, whole, LANES), f32),
        off=pltpu.VMEM((6, whole, LANES), f32),
        inverse=pltpu.VMEM((whole, LANES), f32),
        v=pltpu.VMEM((2, whole, LANES), f32),
        ring_send=pltpu.SemaphoreType.DMA((2, 4)),
        ring_recv=pltpu.SemaphoreType.DMA((2, 4)),
        plane_send=pltpu.SemaphoreType.DMA((2,)),
        plane_recv=pltpu.SemaphoreType.DMA((2,)),
    )
    got = dict(
        table=pltpu.SMEM(class_table.shape, f32),
        source=pltpu.VMEM(flat, f32),
        guess=pltpu.VMEM(flat, f32),
        classes=pltpu.VMEM(flat, jnp.int32),
        sem=pltpu.SemaphoreType.DMA((4,)),
    )
    vmem = pl.BlockSpec(memory_space=pltpu.VMEM)
    solution_out, residual_out = pl.pallas_call(
        functools.partial(kernel, shapes, counts),
        out_shape=[jax.ShapeDtypeStruct(flat, f32)] * 2,
        in_specs=[pl.BlockSpec(memory_space=pltpu.HBM)] * 4,
        out_specs=[vmem, vmem],
        scratch_shapes=[[level_scratch(shapes[0])] + [wide_scratch(shape) for shape in shapes[1:]], co, got],
        compiler_params=pltpu.CompilerParams(
            collective_id=0, has_side_effects=True, vmem_limit_bytes=48 * 1024 * 1024
        ),
        cost_estimate=pl.CostEstimate(flops=100_000_000, bytes_accessed=3_000_000, transcendentals=0),
        name="vcycle",
    )(class_table, source.reshape(flat), first_guess.reshape(flat), cell_classes.reshape(flat))
    return solution_out.reshape(source.shape), residual_out.reshape(source.shape)


def solution(mesh):
    counts = {axis: mesh.shape[axis] for axis in ("gx", "gy", "gz")}
    spec = P("gx", "gy", "gz")
    return jax.shard_map(
        functools.partial(body, counts),
        mesh=mesh,
        in_specs=(spec, spec, spec, P()),
        out_specs=(spec, spec),
        check_vma=False,
    )
```

```python
import functools

import jax
import jax.numpy as jnp
from jax import lax
from jax.experimental import pallas as pl
from jax.experimental.pallas import tpu as pltpu
from jax.sharding import PartitionSpec as P

LEVELS = 3
SWEEPS = 4
COARSE = 16
WEIGHT = 0.85
LANES = 128
PAD = 8
HALO = 4
VMEM_BYTES = 64 * 1024 * 1024
MESH = pl.DeviceIdType.MESH
HIGHEST = lax.Precision.HIGHEST


class Level:
    def __init__(self, index, shape, refs):
        self.index = index
        self.planes, self.rows, self.width = shape
        self.pitch = self.rows + 2 * PAD
        self.scale = 0.25**index
        self.packed = max(self.planes, 8)
        for name, ref in refs.items():
            setattr(self, name, ref)

    def row(self, slot, plane):
        return (slot * (self.planes + 2) + plane) * self.pitch + PAD


def level_scratch(shape):
    planes, rows, _ = shape
    f32 = jnp.float32
    packed = max(planes, 8)
    flat = planes * rows
    return dict(
        v=pltpu.VMEM((3 * (planes + 2) * (rows + 2 * PAD), LANES), f32),
        ysend=pltpu.VMEM((3 * 2 * packed, LANES), f32),
        yrecv=pltpu.VMEM((3 * 2 * packed, LANES), f32),
        zsend=pltpu.VMEM((3 * rows, LANES), f32),
        zrecv=pltpu.VMEM((3 * 2 * rows, LANES), f32),
        edge=pltpu.VMEM((rows, LANES), f32),
        yface=pltpu.VMEM((2 * packed, LANES), f32),
        zface=pltpu.VMEM((rows, LANES), f32),
        off=pltpu.VMEM((6 * flat, LANES), f32),
        rhs=pltpu.VMEM((flat, LANES), f32),
        inverse=pltpu.VMEM((flat, LANES), f32),
        diag=pltpu.VMEM((flat, LANES), f32),
        res=pltpu.VMEM((flat, LANES), f32),
        half=pltpu.VMEM((max(flat // 4, 8), LANES), f32),
        send=pltpu.SemaphoreType.DMA((3, 6)),
        recv=pltpu.SemaphoreType.DMA((3, 6)),
    )


def lanes_of(rows):
    return lax.broadcasted_iota(jnp.int32, (rows, LANES), 1)


def pack(level, plane, values, held):
    lane = lanes_of(values.shape[0])
    first = 2 * plane + 1
    mask = (lane == first) | (lane == ((first + level.width - 1) & (LANES - 1)))
    return jnp.where(mask, pltpu.roll(values, first, 1), held)


def push(level, slot, held, around):
    planes, rows, packed = level.planes, level.rows, level.packed
    level.zsend[pl.ds(slot * rows, rows), :] = held
    for side, row in ((0, 0), (1, rows - 1)):
        level.ysend[pl.ds((slot * 2 + side) * packed, planes), :] = level.v[
            pl.ds(level.row(slot, 1) + row, planes, stride=level.pitch), :
        ]
    own = lambda plane: level.v.at[pl.ds(level.row(slot, plane), rows), :]
    ysend = lambda side: level.ysend.at[pl.ds((slot * 2 + side) * packed, packed), :]
    yrecv = lambda side: level.yrecv.at[pl.ds((slot * 2 + side) * packed, packed), :]
    zsend = level.zsend.at[pl.ds(slot * rows, rows), :]
    zrecv = lambda side: level.zrecv.at[pl.ds((slot * 2 + side) * rows, rows), :]
    plan = (
        (own(planes), own(0), "gx", 1),
        (own(1), own(planes + 1), "gx", -1),
        (ysend(1), yrecv(0), "gy", 1),
        (ysend(0), yrecv(1), "gy", -1),
        (zsend, zrecv(0), "gz", 1),
        (zsend, zrecv(1), "gz", -1),
    )
    copies = []
    for number, (src, dst, axis, step) in enumerate(plan):
        copy = pltpu.make_async_remote_copy(
            src_ref=src,
            dst_ref=dst,
            send_sem=level.send.at[slot, number],
            recv_sem=level.recv.at[slot, number],
            device_id=around(axis, step),
            device_id_type=MESH,
        )
        copy.start()
        copies.append(copy)
    return copies


def pull(level, slot, copies):
    planes, rows, packed, width = level.planes, level.rows, level.packed, level.width
    for copy in copies:
        copy.wait()
    for side, row in ((0, -1), (1, rows)):
        level.v[pl.ds(level.row(slot, 1) + row, planes, stride=level.pitch), :] = level.yrecv[
            pl.ds((slot * 2 + side) * packed, planes), :
        ]
    below = level.zrecv[pl.ds(slot * 2 * rows, rows), :]
    above = level.zrecv[pl.ds((slot * 2 + 1) * rows, rows), :]
    if width < LANES:
        below = pltpu.roll(below, LANES - width, 1)
    above = pltpu.roll(above, width - 2, 1)
    level.edge[...] = jnp.where((lanes_of(rows) & 1) == 0, below, above)


def neighbours(level, slot, plane, center):
    rows, width = level.rows, level.width
    first = level.row(slot, 1) + plane * level.pitch
    at = lambda shift: level.v[pl.ds(first + shift, rows), :]
    lane = lanes_of(rows)
    edge = pltpu.roll(level.edge[...], (LANES - 2 * plane) & (LANES - 1), 1)
    return (
        at(-level.pitch),
        at(level.pitch),
        at(-1),
        at(1),
        jnp.where(lane == 0, edge, pltpu.roll(center, 1, 1)),
        jnp.where(lane == width - 1, edge, pltpu.roll(center, LANES - 1, 1)),
    )


def partial(level, slot, residual):
    rows, planes, flat = level.rows, level.planes, level.planes * level.rows
    held = jnp.zeros((rows, LANES), jnp.float32)
    for plane in range(planes):
        first = level.row(slot, 1) + plane * level.pitch
        at = lambda shift: level.v[pl.ds(first + shift, rows), :]
        off = lambda number: level.off[pl.ds(number * flat + plane * rows, rows), :]
        center = at(0)
        keep = -WEIGHT if residual else 1.0 - WEIGHT
        total = level.rhs[pl.ds(plane * rows, rows), :] + keep * center
        if plane > 0:
            total = total + off(0) * at(-level.pitch)
        if plane < planes - 1:
            total = total + off(1) * at(level.pitch)
        total = total + off(2) * at(-1) + off(3) * at(1)
        total = total + off(4) * pltpu.roll(center, 1, 1) + off(5) * pltpu.roll(center, LANES - 1, 1)
        if residual:
            level.res[pl.ds(plane * rows, rows), :] = total
        else:
            level.v[pl.ds(level.row(1 - slot, 1) + plane * level.pitch, rows), :] = total
            held = pack(level, plane, total, held)
    return held


def arrive(level, slot, copies, ref, base, pitch):
    planes, rows, packed, width = level.planes, level.rows, level.packed, level.width
    flat = planes * rows
    for copy in copies:
        copy.wait()
    for number, plane, there in ((0, 0, 0), (1, planes - 1, planes + 1)):
        at = pl.ds(base + plane * pitch, rows)
        ref[at, :] = ref[at, :] + (
            level.off[pl.ds(number * flat + plane * rows, rows), :]
            * level.v[pl.ds(level.row(slot, there), rows), :]
        )
    for side, row in ((0, 0), (1, rows - 1)):
        at = pl.ds(base + row, planes, stride=pitch)
        ref[at, :] = ref[at, :] + (
            level.yface[pl.ds(side * packed, planes), :]
            * level.yrecv[pl.ds((slot * 2 + side) * packed, planes), :]
        )
    below = level.zrecv[pl.ds(slot * 2 * rows, rows), :]
    above = pltpu.roll(level.zrecv[pl.ds((slot * 2 + 1) * rows, rows), :], width - 2, 1)
    edge = jnp.where((lanes_of(rows) & 1) == 0, below, above) * level.zface[...]
    level.edge[...] = edge
    return edge


def edge_of(level, plane, first, count):
    lane = lanes_of(count)
    shift = (LANES - 2 * plane) & (LANES - 1)
    edge = level.edge[pl.ds(first, count), :]
    moved = pltpu.roll(edge, shift, 1) if shift else edge
    return jnp.where((lane == 0) | (lane == level.width - 1), moved, 0.0)


def close(level, slot, plane, first, count):
    at = pl.ds(level.row(slot, 1) + plane * level.pitch + first, count)
    level.v[at, :] = level.v[at, :] + edge_of(level, plane, first, count)


def join(level, slot, copies, held):
    planes, rows, new = level.planes, level.rows, 1 - slot
    edge = arrive(level, slot, copies, level.v, level.row(new, 1), level.pitch)
    pieces = [(0, 8), (8, rows - 16), (rows - 8, 8)]
    parts = [held[first : first + count] for first, count in pieces]
    for plane in range(planes):
        outer = plane in (0, planes - 1)
        for k, (first, count) in enumerate(pieces):
            if outer or k != 1:
                at = pl.ds(level.row(new, 1) + plane * level.pitch + first, count)
                value = level.v[at, :]
                parts[k] = pack(level, plane, value, parts[k])
                level.v[at, :] = value + edge_of(level, plane, first, count)
    return jnp.concatenate(parts, axis=0) + pltpu.roll(edge, 1, 1)


def rest(level, slot):
    for plane in range(1, level.planes - 1):
        close(level, slot, plane, 8, level.rows - 16)


def complete(level, slot, copies, out):
    rows = level.rows
    arrive(level, slot, copies, level.res, 0, rows)
    for plane in range(level.planes):
        at = pl.ds(plane * rows, rows)
        out[at, :] = (level.res[at, :] + edge_of(level, plane, 0, rows)) * level.diag[at, :]


def smooth(level, slot, held, around, count, between=(), joined=False):
    between = list(between)
    for _ in range(count):
        copies = push(level, slot, held, around)
        if joined:
            rest(level, slot)
        held = partial(level, slot, False)
        if between:
            between.pop(0)()
        held = join(level, slot, copies, held)
        slot, joined = 1 - slot, True
    return slot, held


def restrict(level, read):
    size = level.rows // 2
    for plane in range(level.planes // 2):
        parts = [read(2 * plane + p, q, size) for p in range(2) for q in range(2)]
        level.half[pl.ds(plane * size, size), :] = (parts[0] + parts[1]) + (parts[2] + parts[3])
    row = lax.broadcasted_iota(jnp.int32, (LANES, LANES), 0)
    column = lax.broadcasted_iota(jnp.int32, (LANES, LANES), 1)
    gather = jnp.where((row >> 1) == column, 0.125, 0.0)
    return lax.dot(level.half[...], gather, precision=HIGHEST, preferred_element_type=jnp.float32)


def spread(level, coarse):
    row = lax.broadcasted_iota(jnp.int32, (LANES, LANES), 0)
    column = lax.broadcasted_iota(jnp.int32, (LANES, LANES), 1)
    twice = jnp.where(row == (column >> 1), 1.0, 0.0)
    level.half[...] = lax.dot(coarse, twice, precision=HIGHEST, preferred_element_type=jnp.float32)


def prolong(level, slot, coarse):
    spread(level, coarse)
    size = level.rows // 2
    held = jnp.zeros((level.rows, LANES), jnp.float32)
    for plane in range(level.planes):
        parent = level.half[pl.ds((plane // 2) * size, size), :]
        old, new = level.row(slot, plane + 1), level.row(1 - slot, plane + 1)
        for q in range(2):
            level.v[pl.ds(new + q, size, stride=2), :] = (
                level.v[pl.ds(old + q, size, stride=2), :] + parent
            )
        held = pack(level, plane, level.v[pl.ds(new, level.rows), :], held)
    return held


def coefficients(level, ends):
    rows, planes, width, flat = level.rows, level.planes, level.width, level.planes * level.rows
    lane = lanes_of(rows)
    row = lax.broadcasted_iota(jnp.int32, (rows, LANES), 0)

    never = row < 0
    zface = jnp.zeros((rows, LANES), jnp.float32)
    for plane in range(planes):
        center = level.v[pl.ds(level.row(2, 1) + plane * level.pitch, rows), :]
        outside = (
            ends["gx"][0] if plane == 0 else never,
            ends["gx"][1] if plane == planes - 1 else never,
            (row == 0) & ends["gy"][0],
            (row == rows - 1) & ends["gy"][1],
            (lane == 0) & ends["gz"][0],
            (lane == width - 1) & ends["gz"][1],
        )
        faces = [
            0.5 * (center + jnp.where(out, 0.0, value))
            for out, value in zip(outside, neighbours(level, 2, plane, center), strict=True)
        ]
        diagonal = sum(faces[1:], faces[0])
        inverse = WEIGHT / diagonal
        at = pl.ds(plane * rows, rows)
        level.inverse[at, :] = inverse
        level.diag[at, :] = diagonal * (1.0 / WEIGHT)
        off = [jnp.where(out, 0.0, face * inverse) for out, face in zip(outside, faces, strict=True)]
        level.yface[pl.ds(plane, 1), :] = off[2][:1]
        level.yface[pl.ds(level.packed + plane, 1), :] = off[3][rows - 1 :]
        low = pltpu.roll(off[4], 2 * plane, 1) if plane else off[4]
        high = pltpu.roll(off[5], 2 * plane, 1) if plane else off[5]
        zface = jnp.where(lane == 2 * plane, low, zface)
        zface = jnp.where(lane == ((2 * plane - 1) & (LANES - 1)), high, zface)
        border = (never, never, row == 0, row == rows - 1, lane == 0, lane == width - 1)
        for number in range(6):
            value = off[number] if number < 2 else jnp.where(border[number], 0.0, off[number])
            level.off[pl.ds(number * flat + plane * rows, rows), :] = value
    level.zface[...] = zface


class Wide:
    def __init__(self, index, shape, refs):
        self.index = index
        self.planes, self.rows, self.width = shape
        self.tall = self.rows + 2 * PAD
        self.scale = 0.25**index
        for name, ref in refs.items():
            setattr(self, name, ref)


COEF, RHS, AFTER = 2, 3, 4


def wide_scratch(shape):
    planes, rows, _ = shape
    f32 = jnp.float32
    deep, tall = planes + 2 * HALO, rows + 2 * PAD
    return dict(
        v=pltpu.VMEM((5, deep, tall + 2 * PAD, LANES), f32),
        ends=pltpu.VMEM((3, rows, LANES), f32),
        met=pltpu.VMEM((3, 2, 3, tall, LANES), f32),
        off=pltpu.VMEM((6, deep, tall, LANES), f32),
        inverse=pltpu.VMEM((planes * rows, LANES), f32),
        diag=pltpu.VMEM((planes * rows, LANES), f32),
        res=pltpu.VMEM((planes * rows, LANES), f32),
        half=pltpu.VMEM((planes * rows // 4, LANES), f32),
        send=pltpu.SemaphoreType.DMA((3, 27)),
        recv=pltpu.SemaphoreType.DMA((3, 27)),
    )


def wide_push(level, slot, around):
    planes, rows, width, turn = level.planes, level.rows, level.width, slot - 2
    lane = lanes_of(rows)
    ends = jnp.zeros((rows, LANES), jnp.float32)
    for plane in range(planes):
        low, high = HALO * plane, width - HALO + HALO * plane
        mask = ((lane >= low) & (lane < low + HALO)) | ((lane >= high) & (lane < high + HALO))
        own = level.v[slot, HALO + plane, pl.ds(2 * PAD, rows), :]
        ends = jnp.where(mask, pltpu.roll(own, low, 1) if low else own, ends)
    level.ends[turn] = ends

    def part(step, first, count, size):
        if step == 0:
            return (first, count), (first, count)
        if step > 0:
            return (first + count - size, size), (first - size, size)
        return (first, size), (first + count, size)

    copies = []
    steps = [(a, b, c) for a in (-1, 0, 1) for b in (-1, 0, 1) for c in (-1, 0, 1)]
    for along, across, depth in sorted(steps, key=lambda d: -sum(abs(k) for k in d)):
        (src_x, n_x), (dst_x, _) = part(along, HALO, planes, HALO)
        (src_y, n_y), (dst_y, _) = part(across, PAD, rows, PAD)
        number = (along + 1) * 9 + (across + 1) * 3 + depth + 1
        if number == 13:
            continue
        if depth == 0:
            src = level.v.at[slot, pl.ds(src_x, n_x), pl.ds(PAD + src_y, n_y), :]
            dst = level.v.at[slot, pl.ds(dst_x, n_x), pl.ds(PAD + dst_y, n_y), :]
        else:
            src = level.ends.at[turn, pl.ds(src_y - PAD, n_y), :]
            dst = level.met.at[turn, (1 - depth) // 2, 1 - along, pl.ds(dst_y, n_y), :]
        where = {}
        for axis, step in (("gx", along), ("gy", across), ("gz", depth)):
            if step:
                where.update(around(axis, step))
        copy = pltpu.make_async_remote_copy(
            src_ref=src,
            dst_ref=dst,
            send_sem=level.send.at[turn, number],
            recv_sem=level.recv.at[turn, number],
            device_id=where,
            device_id_type=MESH,
        )
        copy.start()
        copies.append(copy)
    return copies


def wide_pull(level, slot, copies):
    planes, width, tall, turn = level.planes, level.width, level.tall, slot - 2
    lane = lanes_of(tall)
    for copy in copies:
        copy.wait()
    halo = (lane >= LANES - HALO) | ((lane >= width) & (lane < width + HALO))
    for side in range(3):
        below, above = level.met[turn, 0, side], level.met[turn, 1, side]
        if width < LANES // 2:
            below = pltpu.roll(below, LANES - 2 * width, 1)
        both = jnp.where(lane < HALO * planes, above, below)
        first, count, place = (
            (planes - HALO, HALO, 0),
            (0, planes, HALO),
            (0, HALO, HALO + planes),
        )[side]
        for k in range(count):
            shift = (width - HALO * (first + k)) % LANES
            moved = pltpu.roll(both, shift, 1) if shift else both
            old = level.v[slot, place + k, pl.ds(PAD, tall), :]
            level.v[slot, place + k, pl.ds(PAD, tall), :] = jnp.where(halo, moved, old)


def wide_neighbours(level, slot, plane, first, rows):
    at = lambda p, r: level.v[slot, p, pl.ds(r, rows), :]
    center = at(plane, first)
    return center, (
        at(plane - 1, first),
        at(plane + 1, first),
        at(plane, first - 1),
        at(plane, first + 1),
        pltpu.roll(center, 1, 1),
        pltpu.roll(center, LANES - 1, 1),
    )


def wide_change(level, slot, plane, first, rows):
    center, values = wide_neighbours(level, slot, plane, first, rows)
    total = level.v[RHS, plane, pl.ds(first, rows), :] - WEIGHT * center
    for number, value in enumerate(values):
        total = total + level.off[number, plane, pl.ds(first - PAD, rows), :] * value
    return center, total


def wide_sweep(level, slot, into, layers):
    for plane in range(HALO - layers, HALO + level.planes + layers):
        center, total = wide_change(level, slot, plane, PAD, level.tall)
        level.v[into, plane, pl.ds(PAD, level.tall), :] = center + total


def wide_residual(level, slot):
    for plane in range(level.planes):
        at = pl.ds(plane * level.rows, level.rows)
        total = wide_change(level, slot, HALO + plane, 2 * PAD, level.rows)[1]
        level.res[at, :] = total * level.diag[at, :]


def wide_put(level, slot, values):
    for plane in range(level.planes):
        level.v[slot, HALO + plane, pl.ds(2 * PAD, level.rows), :] = values[
            plane * level.rows : (plane + 1) * level.rows, :
        ]


def wide_prolong(level, slot, into, coarse):
    spread(level, coarse)
    size = level.rows // 2
    for plane in range(level.planes):
        parent = level.half[pl.ds((plane // 2) * size, size), :]
        for q in range(2):
            at = pl.ds(2 * PAD + q, size, stride=2)
            level.v[into, HALO + plane, at, :] = level.v[slot, HALO + plane, at, :] + parent


def wide_own(level, slot):
    inside = lanes_of(level.rows) < level.width
    own = [
        jnp.where(inside, level.v[slot, HALO + plane, pl.ds(2 * PAD, level.rows), :], 0.0)
        for plane in range(level.planes)
    ]
    return jnp.concatenate(own, axis=0)


def wide_coefficients(level, ends):
    rows, tall, planes, width = level.rows, level.tall, level.planes, level.width
    lane = lanes_of(tall)
    row = lax.broadcasted_iota(jnp.int32, (tall, LANES), 0)
    never = row < 0
    known = (lane < width + HALO) | (lane >= LANES - HALO)
    inside = lanes_of(rows) < width
    for plane in range(1, planes + 2 * HALO - 1):
        center, values = wide_neighbours(level, COEF, plane, PAD, tall)
        outside = (
            ends["gx"][0] if plane == HALO else never,
            ends["gx"][1] if plane == HALO + planes - 1 else never,
            (row == PAD) & ends["gy"][0],
            (row == PAD + rows - 1) & ends["gy"][1],
            (lane == 0) & ends["gz"][0],
            (lane == width - 1) & ends["gz"][1],
        )
        faces = [
            0.5 * (center + jnp.where(out, 0.0, value))
            for out, value in zip(outside, values, strict=True)
        ]
        diagonal = sum(faces[1:], faces[0])
        inverse = jnp.where(known, WEIGHT / diagonal, 0.0)
        for number in range(6):
            level.off[number, plane] = jnp.where(outside[number], 0.0, faces[number] * inverse)
        if HALO <= plane < HALO + planes:
            at = pl.ds((plane - HALO) * rows, rows)
            own = slice(PAD, PAD + rows)
            level.inverse[at, :] = jnp.where(inside, inverse[own] * (1.0 / level.scale), 0.0)
            level.diag[at, :] = jnp.where(inside, diagonal[own] * (level.scale / WEIGHT), 0.0)


def gather_ring(field, which, co, place, around):
    rows = field.shape[0] // 2
    tile = pltpu.roll(field[:rows, :], place["lane"], 1) + pltpu.roll(
        field[rows:, :], place["lane"] + LANES // 2, 1
    )
    co["tile"][pl.ds(which * 8, 8), :] = tile
    copies = []
    for step in range(1, place["count"]["gz"]):
        copy = pltpu.make_async_remote_copy(
            src_ref=co["tile"].at[pl.ds(which * 8, 8), :],
            dst_ref=co["tiles"].at[pl.ds((which * 4 + step) * 8, 8), :],
            send_sem=co["ring_send"].at[which, step],
            recv_sem=co["ring_recv"].at[which, step],
            device_id=around("gz", step),
            device_id_type=MESH,
        )
        copy.start()
        copies.append(copy)
    return tile, copies


def gather_plane(tile, copies, which, co, place, around):
    for copy in copies:
        copy.wait()
    for step in range(1, place["count"]["gz"]):
        tile = tile + co["tiles"][pl.ds((which * 4 + step) * 8, 8), :]
    mine = co["whole"].at[which, pl.ds(place["row"], 8), :]
    mine[...] = tile
    gx, gy = place["count"]["gx"], place["count"]["gy"]
    others = [(along, across) for along in range(gx) for across in range(gy) if along or across]
    far = lambda step: min(step[0], gx - step[0]) + 2 * min(step[1], gy - step[1])
    for along, across in sorted(others, key=lambda step: -far(step)):
        pltpu.make_async_remote_copy(
            src_ref=mine,
            dst_ref=mine,
            send_sem=co["plane_send"].at[which],
            recv_sem=co["plane_recv"].at[which],
            device_id={**around("gx", along), **around("gy", across)},
            device_id_type=MESH,
        ).start()


def gather_wait(which, co):
    total = co["whole"].shape[1]
    others = co["whole"].at[which, pl.ds(0, total - 8), :]
    pltpu.make_async_copy(others, others, co["plane_send"].at[which]).wait()
    pltpu.make_async_copy(others, others, co["plane_recv"].at[which]).wait()


def coarse_solve(co, scale):
    total = co["whole"].shape[1]
    count, rows = co["whole"].shape[1] // 32, 32
    lane = lanes_of(rows)
    row = lax.broadcasted_iota(jnp.int32, (rows, LANES), 0)
    low = lane < LANES // 2
    depth = lane & (LANES // 2 - 1)

    def around_of(read, group):
        center = read(group)
        swap = lambda g: pltpu.roll(read(g), LANES // 2, 1)
        here = swap(group)
        before = swap(group - 1) if group > 0 else here
        after = swap(group + 1) if group < count - 1 else here
        return center, (
            jnp.where(low, before, here),
            jnp.where(low, here, after),
            pltpu.roll(center, 1, 0),
            pltpu.roll(center, rows - 1, 0),
            pltpu.roll(center, 1, 1),
            pltpu.roll(center, LANES - 1, 1),
        )

    read_coef = lambda g: co["whole"][0, pl.ds(g * rows, rows), :]
    for group in range(count):
        center, values = around_of(read_coef, group)
        never = row < 0
        outside = (
            low if group == 0 else never,
            ~low if group == count - 1 else never,
            row == 0,
            row == rows - 1,
            depth == 0,
            depth == LANES // 2 - 1,
        )
        faces = [
            0.5 * (center + jnp.where(out, 0.0, value))
            for out, value in zip(outside, values, strict=True)
        ]
        diagonal = sum(faces[1:], faces[0])
        inverse = WEIGHT / diagonal
        at = pl.ds(group * rows, rows)
        for number in range(6):
            co["off"][number, at, :] = jnp.where(outside[number], 0.0, faces[number] * inverse)
        co["inverse"][at, :] = inverse * (1.0 / scale)

    yield

    start = co["whole"][1] * co["inverse"][...]
    co["inverse"][...] = start
    co["v"][0] = jnp.zeros((total, LANES), jnp.float32)

    def one(slot):
        read = lambda g: co["v"][slot, pl.ds(g * rows, rows), :]
        for group in range(count):
            center, values = around_of(read, group)
            at = pl.ds(group * rows, rows)
            new = co["inverse"][at, :] + (1.0 - WEIGHT) * center
            for number, value in enumerate(values):
                new = new + co["off"][number, at, :] * value
            co["v"][1 - slot, at, :] = new

    def pair(_, carry):
        one(0)
        one(1)
        return carry

    lax.fori_loop(0, COARSE // 2, pair, 0)


def kernel(shapes, counts, table_in, source_in, guess_in, classes_in, out_u, out_r, refs, co, got):
    table, source, guess, classes = got["table"], got["source"], got["guess"], got["classes"]
    arriving = [
        pltpu.make_async_copy(src, dst, got["sem"].at[number])
        for number, (src, dst) in enumerate(
            ((table_in, table), (classes_in, classes), (guess_in, guess), (source_in, source))
        )
    ]
    for copy in arriving:
        copy.start()
    top = Level(0, shapes[0], refs[0])
    lower = [Wide(index, shapes[index], refs[index]) for index in range(1, len(shapes))]
    position = {axis: lax.axis_index(axis) for axis in counts}

    def around(axis, step):
        count = counts[axis]
        return {axis: lax.rem(position[axis] + (step + count), count)}

    ends = {axis: (position[axis] == 0, position[axis] == counts[axis] - 1) for axis in counts}
    piece = shapes[-1][2] // 2
    place = dict(
        count=counts,
        lane=position["gz"] * piece,
        row=pl.multiple_of(position["gx"] * 32 + position["gy"] * 8, 8),
    )

    partners = set()
    for along in range(counts["gx"]):
        for across in range(counts["gy"]):
            partners.add((along, across, 0))
    for depth in range(counts["gz"]):
        partners.add((0, 0, depth))
    for along in (-1, 0, 1):
        for across in (-1, 0, 1):
            for depth in (-1, 0, 1):
                partners.add((along % counts["gx"], across % counts["gy"], depth % counts["gz"]))
    partners = sorted(partners - {(0, 0, 0)})
    barrier = pltpu.get_barrier_semaphore()
    for along, across, depth in partners:
        where = {**around("gx", along), **around("gy", across), **around("gz", depth)}
        pl.semaphore_signal(barrier, inc=1, device_id=where, device_id_type=MESH)

    for row in (top.row(0, 1) - 1, top.row(0, 1) + top.rows, top.row(1, 1) - 1, top.row(1, 1) + top.rows):
        top.v[pl.ds(row, top.planes, stride=top.pitch), :] = jnp.zeros((top.planes, LANES), jnp.float32)
    for copy in arriving[:3]:
        copy.wait()
    entries = [table[k] for k in range(8)]
    held_c = held_v = jnp.zeros((top.rows, LANES), jnp.float32)
    for plane in range(top.planes):
        at = pl.ds(plane * top.rows, top.rows)
        kind = classes[at, :]
        pick = entries
        for k in range(3):
            bit = (kind & (1 << k)) != 0
            pick = [jnp.where(bit, pick[2 * m + 1], pick[2 * m]) for m in range(len(pick) // 2)]
        values = guess[at, :]
        top.v[pl.ds(top.row(2, 1) + plane * top.pitch, top.rows), :] = pick[0]
        top.v[pl.ds(top.row(0, 1) + plane * top.pitch, top.rows), :] = values
        held_c = pack(top, plane, pick[0], held_c)
        held_v = pack(top, plane, values, held_v)
    pl.semaphore_wait(barrier, len(partners))

    moving = push(top, 2, held_c, around)
    first = push(top, 0, held_v, around)
    coarse = restrict(
        top, lambda plane, q, n: top.v[pl.ds(top.row(2, 1) + plane * top.pitch + q, n, stride=2), :]
    )
    wide_moving = []
    for level in lower:
        wide_put(level, COEF, coarse)
        wide_moving.append(wide_push(level, COEF, around))
        coarse = restrict(
            level,
            lambda plane, q, n: level.v[COEF, HALO + plane, pl.ds(2 * PAD + q, n, stride=2), :],
        )
    tile, copies = gather_ring(coarse, 0, co, place, around)
    pull(top, 2, moving)
    coefficients(top, ends)
    arriving[3].wait()
    top.rhs[...] = source[...] * top.inverse[...]
    held = join(top, 0, first, partial(top, 0, False))

    def ready(level, copies):
        wide_pull(level, COEF, copies)
        wide_coefficients(level, ends)

    solve = coarse_solve(co, 0.25**LEVELS)

    def ready_coarse():
        gather_wait(0, co)
        next(solve)

    between = [functools.partial(gather_plane, tile, copies, 0, co, place, around)]
    between += [functools.partial(ready, *pair) for pair in zip(lower, wide_moving, strict=True)]
    slot, held = smooth(top, 1, held, around, SWEEPS - 1, between, joined=True)
    copies = push(top, slot, held, around)
    rest(top, slot)
    partial(top, slot, True)
    ready_coarse()
    complete(top, slot, copies, top.res)
    fine = slot
    rhs = restrict(top, lambda plane, q, n: top.res[pl.ds(plane * top.rows + q, n, stride=2), :])
    for level in lower:
        wide_put(level, RHS, rhs * level.inverse[...])
        wide_pull(level, RHS, wide_push(level, RHS, around))
        slot = RHS
        for count in range(SWEEPS - 1):
            wide_sweep(level, slot, count % 2, HALO - 1 - count)
            slot = count % 2
        wide_residual(level, slot)
        rhs = restrict(
            level, lambda plane, q, n: level.res[pl.ds(plane * level.rows + q, n, stride=2), :]
        )

    tile, copies = gather_ring(rhs, 1, co, place, around)
    gather_plane(tile, copies, 1, co, place, around)
    gather_wait(1, co)
    next(solve, None)

    mine = co["v"][0, pl.ds(place["row"], 8), :]
    inside = lanes_of(8) < piece
    back = LANES - place["lane"]
    coarse = jnp.concatenate(
        [
            jnp.where(inside, pltpu.roll(mine, back & (LANES - 1), 1), 0.0),
            jnp.where(inside, pltpu.roll(mine, (back + LANES // 2) & (LANES - 1), 1), 0.0),
        ],
        axis=0,
    )
    for level in reversed(lower):
        wide_prolong(level, (SWEEPS - 2) % 2, AFTER, coarse)
        wide_pull(level, AFTER, wide_push(level, AFTER, around))
        slot = AFTER
        for count in range(SWEEPS):
            wide_sweep(level, slot, count % 2, HALO - 1 - count)
            slot = count % 2
        coarse = wide_own(level, slot)
    held = prolong(top, fine, coarse)
    slot, held = smooth(top, 1 - fine, held, around, SWEEPS)
    copies = push(top, slot, held, around)
    rest(top, slot)
    for plane in range(top.planes):
        out_u[pl.ds(plane * top.rows, top.rows), :] = top.v[pl.ds(top.row(slot, plane + 1), top.rows), :]
    partial(top, slot, True)
    complete(top, slot, copies, out_r)


def body(counts, source, first_guess, cell_classes, class_table):
    planes, rows, width = source.shape
    shapes = [(planes >> k, rows >> k, width >> k) for k in range(LEVELS)]
    flat = (planes * rows, width)
    whole = counts["gx"] * 32
    f32 = jnp.float32
    co = dict(
        tile=pltpu.VMEM((2 * 8, LANES), f32),
        tiles=pltpu.VMEM((2 * 4 * 8, LANES), f32),
        whole=pltpu.VMEM((2, whole, LANES), f32),
        off=pltpu.VMEM((6, whole, LANES), f32),
        inverse=pltpu.VMEM((whole, LANES), f32),
        v=pltpu.VMEM((2, whole, LANES), f32),
        ring_send=pltpu.SemaphoreType.DMA((2, 4)),
        ring_recv=pltpu.SemaphoreType.DMA((2, 4)),
        plane_send=pltpu.SemaphoreType.DMA((2,)),
        plane_recv=pltpu.SemaphoreType.DMA((2,)),
    )
    got = dict(
        table=pltpu.SMEM(class_table.shape, f32),
        source=pltpu.VMEM(flat, f32),
        guess=pltpu.VMEM(flat, f32),
        classes=pltpu.VMEM(flat, jnp.int32),
        sem=pltpu.SemaphoreType.DMA((4,)),
    )
    vmem = pl.BlockSpec(memory_space=pltpu.VMEM)
    solution_out, residual_out = pl.pallas_call(
        functools.partial(kernel, shapes, counts),
        out_shape=[jax.ShapeDtypeStruct(flat, f32)] * 2,
        in_specs=[pl.BlockSpec(memory_space=pltpu.HBM)] * 4,
        out_specs=[vmem, vmem],
        scratch_shapes=[[level_scratch(shapes[0])] + [wide_scratch(shape) for shape in shapes[1:]], co, got],
        compiler_params=pltpu.CompilerParams(
            collective_id=0, has_side_effects=True, vmem_limit_bytes=VMEM_BYTES
        ),
        cost_estimate=pl.CostEstimate(flops=100_000_000, bytes_accessed=3_000_000, transcendentals=0),
        name="vcycle",
    )(class_table, source.reshape(flat), first_guess.reshape(flat), cell_classes.reshape(flat))
    return solution_out.reshape(source.shape), residual_out.reshape(source.shape)


def solution(mesh):
    counts = {axis: mesh.shape[axis] for axis in ("gx", "gy", "gz")}
    spec = P("gx", "gy", "gz")
    return jax.shard_map(
        functools.partial(body, counts),
        mesh=mesh,
        in_specs=(spec, spec, spec, P()),
        out_specs=(spec, spec),
        check_vma=False,
    )
```

```python
import functools

import jax
import jax.numpy as jnp
from jax import lax
from jax.experimental import pallas as pl
from jax.experimental.pallas import tpu as pltpu
from jax.sharding import PartitionSpec as P

LEVELS = 3
SWEEPS = 4
COARSE = 16
WEIGHT = 0.85
LANES = 128
PAD = 8
HALO = 4
VMEM_BYTES = 64 * 1024 * 1024
MESH = pl.DeviceIdType.MESH
HIGHEST = lax.Precision.HIGHEST


class Level:
    def __init__(self, index, shape, refs):
        self.index = index
        self.planes, self.rows, self.width = shape
        self.pitch = self.rows + 2 * PAD
        self.scale = 0.25**index
        self.packed = max(self.planes, 8)
        for name, ref in refs.items():
            setattr(self, name, ref)

    def row(self, slot, plane):
        return (slot * (self.planes + 2) + plane) * self.pitch + PAD


def level_scratch(shape):
    planes, rows, _ = shape
    f32 = jnp.float32
    packed = max(planes, 8)
    flat = planes * rows
    return dict(
        v=pltpu.VMEM((3 * (planes + 2) * (rows + 2 * PAD), LANES), f32),
        ysend=pltpu.VMEM((3 * 2 * packed, LANES), f32),
        yrecv=pltpu.VMEM((3 * 2 * packed, LANES), f32),
        zsend=pltpu.VMEM((3 * rows, LANES), f32),
        zrecv=pltpu.VMEM((3 * 2 * rows, LANES), f32),
        edge=pltpu.VMEM((rows, LANES), f32),
        yface=pltpu.VMEM((2 * packed, LANES), f32),
        zface=pltpu.VMEM((rows, LANES), f32),
        off=pltpu.VMEM((6 * flat, LANES), f32),
        rhs=pltpu.VMEM((flat, LANES), f32),
        inverse=pltpu.VMEM((flat, LANES), f32),
        diag=pltpu.VMEM((flat, LANES), f32),
        res=pltpu.VMEM((flat, LANES), f32),
        half=pltpu.VMEM((max(flat // 4, 8), LANES), f32),
        send=pltpu.SemaphoreType.DMA((3, 6)),
        recv=pltpu.SemaphoreType.DMA((3, 6)),
    )


def lanes_of(rows):
    return lax.broadcasted_iota(jnp.int32, (rows, LANES), 1)


def pack(level, plane, values, held):
    lane = lanes_of(values.shape[0])
    first = 2 * plane + 1
    mask = (lane == first) | (lane == ((first + level.width - 1) & (LANES - 1)))
    return jnp.where(mask, pltpu.roll(values, first, 1), held)


def push(level, slot, held, around):
    planes, rows, packed = level.planes, level.rows, level.packed
    level.zsend[pl.ds(slot * rows, rows), :] = held
    for side, row in ((0, 0), (1, rows - 1)):
        level.ysend[pl.ds((slot * 2 + side) * packed, planes), :] = level.v[
            pl.ds(level.row(slot, 1) + row, planes, stride=level.pitch), :
        ]
    own = lambda plane: level.v.at[pl.ds(level.row(slot, plane), rows), :]
    ysend = lambda side: level.ysend.at[pl.ds((slot * 2 + side) * packed, packed), :]
    yrecv = lambda side: level.yrecv.at[pl.ds((slot * 2 + side) * packed, packed), :]
    zsend = level.zsend.at[pl.ds(slot * rows, rows), :]
    zrecv = lambda side: level.zrecv.at[pl.ds((slot * 2 + side) * rows, rows), :]
    plan = (
        (own(planes), own(0), "gx", 1),
        (own(1), own(planes + 1), "gx", -1),
        (ysend(1), yrecv(0), "gy", 1),
        (ysend(0), yrecv(1), "gy", -1),
        (zsend, zrecv(0), "gz", 1),
        (zsend, zrecv(1), "gz", -1),
    )
    copies = []
    for number, (src, dst, axis, step) in enumerate(plan):
        copy = pltpu.make_async_remote_copy(
            src_ref=src,
            dst_ref=dst,
            send_sem=level.send.at[slot, number],
            recv_sem=level.recv.at[slot, number],
            device_id=around(axis, step),
            device_id_type=MESH,
        )
        copy.start()
        copies.append(copy)
    return copies


def pull(level, slot, copies):
    planes, rows, packed, width = level.planes, level.rows, level.packed, level.width
    for copy in copies:
        copy.wait()
    for side, row in ((0, -1), (1, rows)):
        level.v[pl.ds(level.row(slot, 1) + row, planes, stride=level.pitch), :] = level.yrecv[
            pl.ds((slot * 2 + side) * packed, planes), :
        ]
    below = level.zrecv[pl.ds(slot * 2 * rows, rows), :]
    above = level.zrecv[pl.ds((slot * 2 + 1) * rows, rows), :]
    if width < LANES:
        below = pltpu.roll(below, LANES - width, 1)
    above = pltpu.roll(above, width - 2, 1)
    level.edge[...] = jnp.where((lanes_of(rows) & 1) == 0, below, above)


def neighbours(level, slot, plane, center):
    rows, width = level.rows, level.width
    first = level.row(slot, 1) + plane * level.pitch
    at = lambda shift: level.v[pl.ds(first + shift, rows), :]
    lane = lanes_of(rows)
    edge = pltpu.roll(level.edge[...], (LANES - 2 * plane) & (LANES - 1), 1)
    return (
        at(-level.pitch),
        at(level.pitch),
        at(-1),
        at(1),
        jnp.where(lane == 0, edge, pltpu.roll(center, 1, 1)),
        jnp.where(lane == width - 1, edge, pltpu.roll(center, LANES - 1, 1)),
    )


def partial(level, slot, residual):
    rows, planes, flat = level.rows, level.planes, level.planes * level.rows
    held = jnp.zeros((rows, LANES), jnp.float32)
    for plane in range(planes):
        first = level.row(slot, 1) + plane * level.pitch
        at = lambda shift: level.v[pl.ds(first + shift, rows), :]
        off = lambda number: level.off[pl.ds(number * flat + plane * rows, rows), :]
        center = at(0)
        keep = -WEIGHT if residual else 1.0 - WEIGHT
        total = level.rhs[pl.ds(plane * rows, rows), :] + keep * center
        if plane > 0:
            total = total + off(0) * at(-level.pitch)
        if plane < planes - 1:
            total = total + off(1) * at(level.pitch)
        total = total + off(2) * at(-1) + off(3) * at(1)
        total = total + off(4) * pltpu.roll(center, 1, 1) + off(5) * pltpu.roll(center, LANES - 1, 1)
        if residual:
            level.res[pl.ds(plane * rows, rows), :] = total
        else:
            level.v[pl.ds(level.row(1 - slot, 1) + plane * level.pitch, rows), :] = total
            held = pack(level, plane, total, held)
    return held


def arrive(level, slot, copies, ref, base, pitch):
    planes, rows, packed, width = level.planes, level.rows, level.packed, level.width
    flat = planes * rows
    for copy in copies:
        copy.wait()
    for number, plane, there in ((0, 0, 0), (1, planes - 1, planes + 1)):
        at = pl.ds(base + plane * pitch, rows)
        ref[at, :] = ref[at, :] + (
            level.off[pl.ds(number * flat + plane * rows, rows), :]
            * level.v[pl.ds(level.row(slot, there), rows), :]
        )
    for side, row in ((0, 0), (1, rows - 1)):
        at = pl.ds(base + row, planes, stride=pitch)
        ref[at, :] = ref[at, :] + (
            level.yface[pl.ds(side * packed, planes), :]
            * level.yrecv[pl.ds((slot * 2 + side) * packed, planes), :]
        )
    below = level.zrecv[pl.ds(slot * 2 * rows, rows), :]
    above = pltpu.roll(level.zrecv[pl.ds((slot * 2 + 1) * rows, rows), :], width - 2, 1)
    edge = jnp.where((lanes_of(rows) & 1) == 0, below, above) * level.zface[...]
    level.edge[...] = edge
    return edge


def edge_of(level, plane, first, count):
    lane = lanes_of(count)
    shift = (LANES - 2 * plane) & (LANES - 1)
    edge = level.edge[pl.ds(first, count), :]
    moved = pltpu.roll(edge, shift, 1) if shift else edge
    return jnp.where((lane == 0) | (lane == level.width - 1), moved, 0.0)


def close(level, slot, plane, first, count):
    at = pl.ds(level.row(slot, 1) + plane * level.pitch + first, count)
    level.v[at, :] = level.v[at, :] + edge_of(level, plane, first, count)


def join(level, slot, copies, held):
    planes, rows, new = level.planes, level.rows, 1 - slot
    edge = arrive(level, slot, copies, level.v, level.row(new, 1), level.pitch)
    pieces = [(0, 8), (8, rows - 16), (rows - 8, 8)]
    parts = [held[first : first + count] for first, count in pieces]
    for plane in range(planes):
        outer = plane in (0, planes - 1)
        for k, (first, count) in enumerate(pieces):
            if outer or k != 1:
                at = pl.ds(level.row(new, 1) + plane * level.pitch + first, count)
                value = level.v[at, :]
                parts[k] = pack(level, plane, value, parts[k])
                level.v[at, :] = value + edge_of(level, plane, first, count)
    return jnp.concatenate(parts, axis=0) + pltpu.roll(edge, 1, 1)


def rest(level, slot):
    for plane in range(1, level.planes - 1):
        close(level, slot, plane, 8, level.rows - 16)


def complete(level, slot, copies, out):
    rows = level.rows
    arrive(level, slot, copies, level.res, 0, rows)
    for plane in range(level.planes):
        at = pl.ds(plane * rows, rows)
        out[at, :] = (level.res[at, :] + edge_of(level, plane, 0, rows)) * level.diag[at, :]


def smooth(level, slot, held, around, count, between=(), joined=False):
    between = list(between)
    for _ in range(count):
        copies = push(level, slot, held, around)
        if joined:
            rest(level, slot)
        held = partial(level, slot, False)
        if between:
            between.pop(0)()
        held = join(level, slot, copies, held)
        slot, joined = 1 - slot, True
    return slot, held


def restrict(level, read):
    size = level.rows // 2
    for plane in range(level.planes // 2):
        parts = [read(2 * plane + p, q, size) for p in range(2) for q in range(2)]
        level.half[pl.ds(plane * size, size), :] = (parts[0] + parts[1]) + (parts[2] + parts[3])
    row = lax.broadcasted_iota(jnp.int32, (LANES, LANES), 0)
    column = lax.broadcasted_iota(jnp.int32, (LANES, LANES), 1)
    gather = jnp.where((row >> 1) == column, 0.125, 0.0)
    return lax.dot(level.half[...], gather, precision=HIGHEST, preferred_element_type=jnp.float32)


def spread(level, coarse):
    row = lax.broadcasted_iota(jnp.int32, (LANES, LANES), 0)
    column = lax.broadcasted_iota(jnp.int32, (LANES, LANES), 1)
    twice = jnp.where(row == (column >> 1), 1.0, 0.0)
    level.half[...] = lax.dot(coarse, twice, precision=HIGHEST, preferred_element_type=jnp.float32)


def prolong(level, slot, coarse):
    spread(level, coarse)
    size = level.rows // 2
    held = jnp.zeros((level.rows, LANES), jnp.float32)
    for plane in range(level.planes):
        parent = level.half[pl.ds((plane // 2) * size, size), :]
        old, new = level.row(slot, plane + 1), level.row(1 - slot, plane + 1)
        for q in range(2):
            level.v[pl.ds(new + q, size, stride=2), :] = (
                level.v[pl.ds(old + q, size, stride=2), :] + parent
            )
        held = pack(level, plane, level.v[pl.ds(new, level.rows), :], held)
    return held


def coefficients(level, ends):
    rows, planes, width, flat = level.rows, level.planes, level.width, level.planes * level.rows
    lane = lanes_of(rows)
    row = lax.broadcasted_iota(jnp.int32, (rows, LANES), 0)

    never = row < 0
    zface = jnp.zeros((rows, LANES), jnp.float32)
    for plane in range(planes):
        center = level.v[pl.ds(level.row(2, 1) + plane * level.pitch, rows), :]
        outside = (
            ends["gx"][0] if plane == 0 else never,
            ends["gx"][1] if plane == planes - 1 else never,
            (row == 0) & ends["gy"][0],
            (row == rows - 1) & ends["gy"][1],
            (lane == 0) & ends["gz"][0],
            (lane == width - 1) & ends["gz"][1],
        )
        faces = [
            0.5 * (center + jnp.where(out, 0.0, value))
            for out, value in zip(outside, neighbours(level, 2, plane, center), strict=True)
        ]
        diagonal = sum(faces[1:], faces[0])
        inverse = WEIGHT / diagonal
        at = pl.ds(plane * rows, rows)
        level.inverse[at, :] = inverse
        level.diag[at, :] = diagonal * (1.0 / WEIGHT)
        off = [jnp.where(out, 0.0, face * inverse) for out, face in zip(outside, faces, strict=True)]
        level.yface[pl.ds(plane, 1), :] = off[2][:1]
        level.yface[pl.ds(level.packed + plane, 1), :] = off[3][rows - 1 :]
        low = pltpu.roll(off[4], 2 * plane, 1) if plane else off[4]
        high = pltpu.roll(off[5], 2 * plane, 1) if plane else off[5]
        zface = jnp.where(lane == 2 * plane, low, zface)
        zface = jnp.where(lane == ((2 * plane - 1) & (LANES - 1)), high, zface)
        border = (never, never, row == 0, row == rows - 1, lane == 0, lane == width - 1)
        for number in range(6):
            value = off[number] if number < 2 else jnp.where(border[number], 0.0, off[number])
            level.off[pl.ds(number * flat + plane * rows, rows), :] = value
    level.zface[...] = zface


class Wide:
    def __init__(self, index, shape, refs):
        self.index = index
        self.planes, self.rows, self.width = shape
        self.tall = self.rows + 2 * PAD
        self.scale = 0.25**index
        for name, ref in refs.items():
            setattr(self, name, ref)


COEF, RHS, AFTER = 2, 3, 4


def wide_scratch(shape):
    planes, rows, _ = shape
    f32 = jnp.float32
    deep, tall = planes + 2 * HALO, rows + 2 * PAD
    return dict(
        v=pltpu.VMEM((5, deep, tall + 2 * PAD, LANES), f32),
        ends=pltpu.VMEM((3, rows, LANES), f32),
        met=pltpu.VMEM((3, 2, 3, tall, LANES), f32),
        off=pltpu.VMEM((6, deep, tall, LANES), f32),
        inverse=pltpu.VMEM((planes * rows, LANES), f32),
        diag=pltpu.VMEM((planes * rows, LANES), f32),
        res=pltpu.VMEM((planes * rows, LANES), f32),
        half=pltpu.VMEM((planes * rows // 4, LANES), f32),
        send=pltpu.SemaphoreType.DMA((3, 27)),
        recv=pltpu.SemaphoreType.DMA((3, 27)),
    )


def wide_push(level, slot, around):
    planes, rows, width, turn = level.planes, level.rows, level.width, slot - 2
    lane = lanes_of(rows)
    ends = jnp.zeros((rows, LANES), jnp.float32)
    for plane in range(planes):
        low, high = HALO * plane, width - HALO + HALO * plane
        mask = ((lane >= low) & (lane < low + HALO)) | ((lane >= high) & (lane < high + HALO))
        own = level.v[slot, HALO + plane, pl.ds(2 * PAD, rows), :]
        ends = jnp.where(mask, pltpu.roll(own, low, 1) if low else own, ends)
    level.ends[turn] = ends

    def part(step, first, count, size):
        if step == 0:
            return (first, count), (first, count)
        if step > 0:
            return (first + count - size, size), (first - size, size)
        return (first, size), (first + count, size)

    copies = []
    steps = [(a, b, c) for a in (-1, 0, 1) for b in (-1, 0, 1) for c in (-1, 0, 1)]
    for along, across, depth in sorted(steps, key=lambda d: -sum(abs(k) for k in d)):
        (src_x, n_x), (dst_x, _) = part(along, HALO, planes, HALO)
        (src_y, n_y), (dst_y, _) = part(across, PAD, rows, PAD)
        number = (along + 1) * 9 + (across + 1) * 3 + depth + 1
        if number == 13:
            continue
        if depth == 0:
            src = level.v.at[slot, pl.ds(src_x, n_x), pl.ds(PAD + src_y, n_y), :]
            dst = level.v.at[slot, pl.ds(dst_x, n_x), pl.ds(PAD + dst_y, n_y), :]
        else:
            src = level.ends.at[turn, pl.ds(src_y - PAD, n_y), :]
            dst = level.met.at[turn, (1 - depth) // 2, 1 - along, pl.ds(dst_y, n_y), :]
        where = {}
        for axis, step in (("gx", along), ("gy", across), ("gz", depth)):
            if step:
                where.update(around(axis, step))
        copy = pltpu.make_async_remote_copy(
            src_ref=src,
            dst_ref=dst,
            send_sem=level.send.at[turn, number],
            recv_sem=level.recv.at[turn, number],
            device_id=where,
            device_id_type=MESH,
        )
        copy.start()
        copies.append(copy)
    return copies


def wide_pull(level, slot, copies):
    planes, width, tall, turn = level.planes, level.width, level.tall, slot - 2
    lane = lanes_of(tall)
    for copy in copies:
        copy.wait()
    halo = (lane >= LANES - HALO) | ((lane >= width) & (lane < width + HALO))
    for side in range(3):
        below, above = level.met[turn, 0, side], level.met[turn, 1, side]
        if width < LANES // 2:
            below = pltpu.roll(below, LANES - 2 * width, 1)
        both = jnp.where(lane < HALO * planes, above, below)
        first, count, place = (
            (planes - HALO, HALO, 0),
            (0, planes, HALO),
            (0, HALO, HALO + planes),
        )[side]
        for k in range(count):
            shift = (width - HALO * (first + k)) % LANES
            moved = pltpu.roll(both, shift, 1) if shift else both
            old = level.v[slot, place + k, pl.ds(PAD, tall), :]
            level.v[slot, place + k, pl.ds(PAD, tall), :] = jnp.where(halo, moved, old)


def wide_neighbours(level, slot, plane, first, rows):
    at = lambda p, r: level.v[slot, p, pl.ds(r, rows), :]
    center = at(plane, first)
    return center, (
        at(plane - 1, first),
        at(plane + 1, first),
        at(plane, first - 1),
        at(plane, first + 1),
        pltpu.roll(center, 1, 1),
        pltpu.roll(center, LANES - 1, 1),
    )


def wide_change(level, slot, plane, first, rows):
    center, values = wide_neighbours(level, slot, plane, first, rows)
    total = level.v[RHS, plane, pl.ds(first, rows), :] - WEIGHT * center
    for number, value in enumerate(values):
        total = total + level.off[number, plane, pl.ds(first - PAD, rows), :] * value
    return center, total


def wide_sweep(level, slot, into, layers):
    for plane in range(HALO - layers, HALO + level.planes + layers):
        center, total = wide_change(level, slot, plane, PAD, level.tall)
        level.v[into, plane, pl.ds(PAD, level.tall), :] = center + total


def wide_residual(level, slot):
    for plane in range(level.planes):
        at = pl.ds(plane * level.rows, level.rows)
        total = wide_change(level, slot, HALO + plane, 2 * PAD, level.rows)[1]
        level.res[at, :] = total * level.diag[at, :]


def wide_put(level, slot, values):
    for plane in range(level.planes):
        level.v[slot, HALO + plane, pl.ds(2 * PAD, level.rows), :] = values[
            plane * level.rows : (plane + 1) * level.rows, :
        ]


def wide_prolong(level, slot, into, coarse):
    spread(level, coarse)
    size = level.rows // 2
    for plane in range(level.planes):
        parent = level.half[pl.ds((plane // 2) * size, size), :]
        for q in range(2):
            at = pl.ds(2 * PAD + q, size, stride=2)
            level.v[into, HALO + plane, at, :] = level.v[slot, HALO + plane, at, :] + parent


def wide_own(level, slot):
    inside = lanes_of(level.rows) < level.width
    own = [
        jnp.where(inside, level.v[slot, HALO + plane, pl.ds(2 * PAD, level.rows), :], 0.0)
        for plane in range(level.planes)
    ]
    return jnp.concatenate(own, axis=0)


def wide_coefficients(level, ends):
    rows, tall, planes, width = level.rows, level.tall, level.planes, level.width
    lane = lanes_of(tall)
    row = lax.broadcasted_iota(jnp.int32, (tall, LANES), 0)
    never = row < 0
    known = (lane < width + HALO) | (lane >= LANES - HALO)
    inside = lanes_of(rows) < width
    for plane in range(1, planes + 2 * HALO - 1):
        center, values = wide_neighbours(level, COEF, plane, PAD, tall)
        outside = (
            ends["gx"][0] if plane == HALO else never,
            ends["gx"][1] if plane == HALO + planes - 1 else never,
            (row == PAD) & ends["gy"][0],
            (row == PAD + rows - 1) & ends["gy"][1],
            (lane == 0) & ends["gz"][0],
            (lane == width - 1) & ends["gz"][1],
        )
        faces = [
            0.5 * (center + jnp.where(out, 0.0, value))
            for out, value in zip(outside, values, strict=True)
        ]
        diagonal = sum(faces[1:], faces[0])
        inverse = jnp.where(known, WEIGHT / diagonal, 0.0)
        for number in range(6):
            level.off[number, plane] = jnp.where(outside[number], 0.0, faces[number] * inverse)
        if HALO <= plane < HALO + planes:
            at = pl.ds((plane - HALO) * rows, rows)
            own = slice(PAD, PAD + rows)
            level.inverse[at, :] = jnp.where(inside, inverse[own] * (1.0 / level.scale), 0.0)
            level.diag[at, :] = jnp.where(inside, diagonal[own] * (level.scale / WEIGHT), 0.0)


def gather_ring(field, which, co, place, around):
    rows = field.shape[0] // 2
    tile = pltpu.roll(field[:rows, :], place["lane"], 1) + pltpu.roll(
        field[rows:, :], place["lane"] + LANES // 2, 1
    )
    co["tile"][pl.ds(which * 8, 8), :] = tile
    copies = []
    for step in range(1, place["count"]["gz"]):
        copy = pltpu.make_async_remote_copy(
            src_ref=co["tile"].at[pl.ds(which * 8, 8), :],
            dst_ref=co["tiles"].at[pl.ds((which * 4 + step) * 8, 8), :],
            send_sem=co["ring_send"].at[which, step],
            recv_sem=co["ring_recv"].at[which, step],
            device_id=around("gz", step),
            device_id_type=MESH,
        )
        copy.start()
        copies.append(copy)
    return tile, copies


def gather_plane(tile, copies, which, co, place, around):
    for copy in copies:
        copy.wait()
    for step in range(1, place["count"]["gz"]):
        tile = tile + co["tiles"][pl.ds((which * 4 + step) * 8, 8), :]
    mine = co["whole"].at[which, pl.ds(place["row"], 8), :]
    mine[...] = tile
    gx, gy = place["count"]["gx"], place["count"]["gy"]
    others = [(along, across) for along in range(gx) for across in range(gy) if along or across]
    far = lambda step: min(step[0], gx - step[0]) + 2 * min(step[1], gy - step[1])
    for along, across in sorted(others, key=lambda step: -far(step)):
        pltpu.make_async_remote_copy(
            src_ref=mine,
            dst_ref=mine,
            send_sem=co["plane_send"].at[which],
            recv_sem=co["plane_recv"].at[which],
            device_id={**around("gx", along), **around("gy", across)},
            device_id_type=MESH,
        ).start()


def gather_wait(which, co):
    total = co["whole"].shape[1]
    others = co["whole"].at[which, pl.ds(0, total - 8), :]
    pltpu.make_async_copy(others, others, co["plane_send"].at[which]).wait()
    pltpu.make_async_copy(others, others, co["plane_recv"].at[which]).wait()


def coarse_solve(co, scale):
    total = co["whole"].shape[1]
    count, rows = co["whole"].shape[1] // 32, 32
    lane = lanes_of(rows)
    row = lax.broadcasted_iota(jnp.int32, (rows, LANES), 0)
    low = lane < LANES // 2
    depth = lane & (LANES // 2 - 1)

    def around_of(read, group):
        center = read(group)
        swap = lambda g: pltpu.roll(read(g), LANES // 2, 1)
        here = swap(group)
        before = swap(group - 1) if group > 0 else here
        after = swap(group + 1) if group < count - 1 else here
        return center, (
            jnp.where(low, before, here),
            jnp.where(low, here, after),
            pltpu.roll(center, 1, 0),
            pltpu.roll(center, rows - 1, 0),
            pltpu.roll(center, 1, 1),
            pltpu.roll(center, LANES - 1, 1),
        )

    read_coef = lambda g: co["whole"][0, pl.ds(g * rows, rows), :]
    for group in range(count):
        center, values = around_of(read_coef, group)
        never = row < 0
        outside = (
            low if group == 0 else never,
            ~low if group == count - 1 else never,
            row == 0,
            row == rows - 1,
            depth == 0,
            depth == LANES // 2 - 1,
        )
        faces = [
            0.5 * (center + jnp.where(out, 0.0, value))
            for out, value in zip(outside, values, strict=True)
        ]
        diagonal = sum(faces[1:], faces[0])
        inverse = WEIGHT / diagonal
        at = pl.ds(group * rows, rows)
        for number in range(6):
            co["off"][number, at, :] = jnp.where(outside[number], 0.0, faces[number] * inverse)
        co["inverse"][at, :] = inverse * (1.0 / scale)

    yield

    start = co["whole"][1] * co["inverse"][...]
    co["inverse"][...] = start
    co["v"][0] = jnp.zeros((total, LANES), jnp.float32)

    def one(slot):
        read = lambda g: co["v"][slot, pl.ds(g * rows, rows), :]
        for group in range(count):
            center, values = around_of(read, group)
            at = pl.ds(group * rows, rows)
            new = co["inverse"][at, :] + (1.0 - WEIGHT) * center
            for number, value in enumerate(values):
                new = new + co["off"][number, at, :] * value
            co["v"][1 - slot, at, :] = new

    def pair(_, carry):
        one(0)
        one(1)
        return carry

    lax.fori_loop(0, COARSE // 2, pair, 0)


def kernel(shapes, counts, table_in, source_in, guess_in, classes_in, out_u, out_r, refs, co, got):
    table, source, guess, classes = got["table"], got["source"], got["guess"], got["classes"]
    arriving = [
        pltpu.make_async_copy(src, dst, got["sem"].at[number])
        for number, (src, dst) in enumerate(
            ((table_in, table), (classes_in, classes), (guess_in, guess), (source_in, source))
        )
    ]
    for copy in arriving:
        copy.start()
    top = Level(0, shapes[0], refs[0])
    lower = [Wide(index, shapes[index], refs[index]) for index in range(1, len(shapes))]
    position = {axis: lax.axis_index(axis) for axis in counts}

    def around(axis, step):
        count = counts[axis]
        return {axis: lax.rem(position[axis] + (step + count), count)}

    ends = {axis: (position[axis] == 0, position[axis] == counts[axis] - 1) for axis in counts}
    piece = shapes[-1][2] // 2
    place = dict(
        count=counts,
        lane=position["gz"] * piece,
        row=pl.multiple_of(position["gx"] * 32 + position["gy"] * 8, 8),
    )

    partners = [(axis, step) for axis in counts for step in (-1, 1)]
    barrier = pltpu.get_barrier_semaphore()
    for axis, step in partners:
        pl.semaphore_signal(barrier, inc=1, device_id=around(axis, step), device_id_type=MESH)

    for row in (top.row(0, 1) - 1, top.row(0, 1) + top.rows, top.row(1, 1) - 1, top.row(1, 1) + top.rows):
        top.v[pl.ds(row, top.planes, stride=top.pitch), :] = jnp.zeros((top.planes, LANES), jnp.float32)
    for copy in arriving[:3]:
        copy.wait()
    entries = [table[k] for k in range(8)]
    held_c = held_v = jnp.zeros((top.rows, LANES), jnp.float32)
    for plane in range(top.planes):
        at = pl.ds(plane * top.rows, top.rows)
        kind = classes[at, :]
        pick = entries
        for k in range(3):
            bit = (kind & (1 << k)) != 0
            pick = [jnp.where(bit, pick[2 * m + 1], pick[2 * m]) for m in range(len(pick) // 2)]
        values = guess[at, :]
        top.v[pl.ds(top.row(2, 1) + plane * top.pitch, top.rows), :] = pick[0]
        top.v[pl.ds(top.row(0, 1) + plane * top.pitch, top.rows), :] = values
        held_c = pack(top, plane, pick[0], held_c)
        held_v = pack(top, plane, values, held_v)
    pl.semaphore_wait(barrier, len(partners))

    moving = push(top, 2, held_c, around)
    first = push(top, 0, held_v, around)
    coarse = restrict(
        top, lambda plane, q, n: top.v[pl.ds(top.row(2, 1) + plane * top.pitch + q, n, stride=2), :]
    )
    for level in lower:
        wide_put(level, COEF, coarse)
        coarse = restrict(
            level,
            lambda plane, q, n: level.v[COEF, HALO + plane, pl.ds(2 * PAD + q, n, stride=2), :],
        )
    pull(top, 2, moving)
    tile, ring = gather_ring(coarse, 0, co, place, around)
    coefficients(top, ends)
    arriving[3].wait()
    top.rhs[...] = source[...] * top.inverse[...]
    held = join(top, 0, first, partial(top, 0, False))

    wide_moving = {}

    def depart():
        for level in lower:
            wide_moving[level.index] = wide_push(level, COEF, around)

    def ready(level):
        wide_pull(level, COEF, wide_moving[level.index])
        wide_coefficients(level, ends)

    solve = coarse_solve(co, 0.25**LEVELS)

    def ready_coarse():
        gather_wait(0, co)
        next(solve)

    between = [lambda: None, depart, functools.partial(ready, lower[0])]
    slot, held = smooth(top, 1, held, around, SWEEPS - 1, between, joined=True)
    copies = push(top, slot, held, around)
    rest(top, slot)
    partial(top, slot, True)
    for level in lower[1:]:
        ready(level)
    complete(top, slot, copies, top.res)
    fine = slot
    rhs = restrict(top, lambda plane, q, n: top.res[pl.ds(plane * top.rows + q, n, stride=2), :])
    for level in lower:
        wide_put(level, RHS, rhs * level.inverse[...])
        copies = wide_push(level, RHS, around)
        if level is lower[0]:
            gather_plane(tile, ring, 0, co, place, around)
        if level is lower[-1]:
            ready_coarse()
        wide_pull(level, RHS, copies)
        slot = RHS
        for count in range(SWEEPS - 1):
            wide_sweep(level, slot, count % 2, HALO - 1 - count)
            slot = count % 2
        wide_residual(level, slot)
        rhs = restrict(
            level, lambda plane, q, n: level.res[pl.ds(plane * level.rows + q, n, stride=2), :]
        )

    tile, copies = gather_ring(rhs, 1, co, place, around)
    gather_plane(tile, copies, 1, co, place, around)
    gather_wait(1, co)
    next(solve, None)

    mine = co["v"][0, pl.ds(place["row"], 8), :]
    inside = lanes_of(8) < piece
    back = LANES - place["lane"]
    coarse = jnp.concatenate(
        [
            jnp.where(inside, pltpu.roll(mine, back & (LANES - 1), 1), 0.0),
            jnp.where(inside, pltpu.roll(mine, (back + LANES // 2) & (LANES - 1), 1), 0.0),
        ],
        axis=0,
    )
    for level in reversed(lower):
        wide_prolong(level, (SWEEPS - 2) % 2, AFTER, coarse)
        wide_pull(level, AFTER, wide_push(level, AFTER, around))
        slot = AFTER
        for count in range(SWEEPS):
            wide_sweep(level, slot, count % 2, HALO - 1 - count)
            slot = count % 2
        coarse = wide_own(level, slot)
    held = prolong(top, fine, coarse)
    slot, held = smooth(top, 1 - fine, held, around, SWEEPS)
    copies = push(top, slot, held, around)
    rest(top, slot)
    for plane in range(top.planes):
        out_u[pl.ds(plane * top.rows, top.rows), :] = top.v[pl.ds(top.row(slot, plane + 1), top.rows), :]
    partial(top, slot, True)
    complete(top, slot, copies, out_r)


def body(counts, source, first_guess, cell_classes, class_table):
    planes, rows, width = source.shape
    shapes = [(planes >> k, rows >> k, width >> k) for k in range(LEVELS)]
    flat = (planes * rows, width)
    whole = counts["gx"] * 32
    f32 = jnp.float32
    co = dict(
        tile=pltpu.VMEM((2 * 8, LANES), f32),
        tiles=pltpu.VMEM((2 * 4 * 8, LANES), f32),
        whole=pltpu.VMEM((2, whole, LANES), f32),
        off=pltpu.VMEM((6, whole, LANES), f32),
        inverse=pltpu.VMEM((whole, LANES), f32),
        v=pltpu.VMEM((2, whole, LANES), f32),
        ring_send=pltpu.SemaphoreType.DMA((2, 4)),
        ring_recv=pltpu.SemaphoreType.DMA((2, 4)),
        plane_send=pltpu.SemaphoreType.DMA((2,)),
        plane_recv=pltpu.SemaphoreType.DMA((2,)),
    )
    got = dict(
        table=pltpu.SMEM(class_table.shape, f32),
        source=pltpu.VMEM(flat, f32),
        guess=pltpu.VMEM(flat, f32),
        classes=pltpu.VMEM(flat, jnp.int32),
        sem=pltpu.SemaphoreType.DMA((4,)),
    )
    vmem = pl.BlockSpec(memory_space=pltpu.VMEM)
    solution_out, residual_out = pl.pallas_call(
        functools.partial(kernel, shapes, counts),
        out_shape=[jax.ShapeDtypeStruct(flat, f32)] * 2,
        in_specs=[pl.BlockSpec(memory_space=pltpu.HBM)] * 4,
        out_specs=[vmem, vmem],
        scratch_shapes=[[level_scratch(shapes[0])] + [wide_scratch(shape) for shape in shapes[1:]], co, got],
        compiler_params=pltpu.CompilerParams(
            collective_id=0, has_side_effects=True, vmem_limit_bytes=VMEM_BYTES
        ),
        cost_estimate=pl.CostEstimate(flops=100_000_000, bytes_accessed=3_000_000, transcendentals=0),
        name="vcycle",
    )(class_table, source.reshape(flat), first_guess.reshape(flat), cell_classes.reshape(flat))
    return solution_out.reshape(source.shape), residual_out.reshape(source.shape)


def solution(mesh):
    counts = {axis: mesh.shape[axis] for axis in ("gx", "gy", "gz")}
    spec = P("gx", "gy", "gz")
    return jax.shard_map(
        functools.partial(body, counts),
        mesh=mesh,
        in_specs=(spec, spec, spec, P()),
        out_specs=(spec, spec),
        check_vma=False,
    )
```

```python
import functools

import jax
import jax.numpy as jnp
from jax import lax
from jax.experimental import pallas as pl
from jax.experimental.pallas import tpu as pltpu
from jax.sharding import PartitionSpec as P

LEVELS = 3
SWEEPS = 4
COARSE = 16
WEIGHT = 0.85
LANES = 128
PAD = 8
HALO = 4
MARGIN = 40
VMEM_BYTES = 64 * 1024 * 1024
MESH = pl.DeviceIdType.MESH
HIGHEST = lax.Precision.HIGHEST


class Level:
    def __init__(self, index, shape, refs):
        self.index = index
        self.planes, self.rows, self.width = shape
        self.pitch = self.rows + 2 * PAD
        self.scale = 0.25**index
        self.packed = max(self.planes, 8)
        for name, ref in refs.items():
            setattr(self, name, ref)

    def row(self, slot, plane):
        return (slot * (self.planes + 2) + plane) * self.pitch + PAD


def level_scratch(shape):
    planes, rows, _ = shape
    f32 = jnp.float32
    packed = max(planes, 8)
    flat = planes * rows
    return dict(
        v=pltpu.VMEM((3 * (planes + 2) * (rows + 2 * PAD), LANES), f32),
        ysend=pltpu.VMEM((3 * 2 * packed, LANES), f32),
        yrecv=pltpu.VMEM((3 * 2 * packed, LANES), f32),
        zsend=pltpu.VMEM((3 * rows, LANES), f32),
        zrecv=pltpu.VMEM((3 * 2 * rows, LANES), f32),
        edge=pltpu.VMEM((rows, LANES), f32),
        yface=pltpu.VMEM((2 * packed, LANES), f32),
        zface=pltpu.VMEM((rows, LANES), f32),
        off=pltpu.VMEM((6 * flat, LANES), f32),
        rhs=pltpu.VMEM((flat, LANES), f32),
        inverse=pltpu.VMEM((flat, LANES), f32),
        diag=pltpu.VMEM((flat, LANES), f32),
        res=pltpu.VMEM((flat, LANES), f32),
        half=pltpu.VMEM((max(flat // 4, 8), LANES), f32),
        send=pltpu.SemaphoreType.DMA((3, 6)),
        recv=pltpu.SemaphoreType.DMA((3, 6)),
    )


def lanes_of(rows):
    return lax.broadcasted_iota(jnp.int32, (rows, LANES), 1)


def pack(level, plane, values, held):
    lane = lanes_of(values.shape[0])
    first = 2 * plane + 1
    mask = (lane == first) | (lane == ((first + level.width - 1) & (LANES - 1)))
    return jnp.where(mask, pltpu.roll(values, first, 1), held)


def push(level, slot, held, around):
    planes, rows, packed = level.planes, level.rows, level.packed
    level.zsend[pl.ds(slot * rows, rows), :] = held
    for side, row in ((0, 0), (1, rows - 1)):
        level.ysend[pl.ds((slot * 2 + side) * packed, planes), :] = level.v[
            pl.ds(level.row(slot, 1) + row, planes, stride=level.pitch), :
        ]
    own = lambda plane: level.v.at[pl.ds(level.row(slot, plane), rows), :]
    ysend = lambda side: level.ysend.at[pl.ds((slot * 2 + side) * packed, packed), :]
    yrecv = lambda side: level.yrecv.at[pl.ds((slot * 2 + side) * packed, packed), :]
    zsend = level.zsend.at[pl.ds(slot * rows, rows), :]
    zrecv = lambda side: level.zrecv.at[pl.ds((slot * 2 + side) * rows, rows), :]
    plan = (
        (own(planes), own(0), "gx", 1),
        (own(1), own(planes + 1), "gx", -1),
        (ysend(1), yrecv(0), "gy", 1),
        (ysend(0), yrecv(1), "gy", -1),
        (zsend, zrecv(0), "gz", 1),
        (zsend, zrecv(1), "gz", -1),
    )
    copies = []
    for number, (src, dst, axis, step) in enumerate(plan):
        copy = pltpu.make_async_remote_copy(
            src_ref=src,
            dst_ref=dst,
            send_sem=level.send.at[slot, number],
            recv_sem=level.recv.at[slot, number],
            device_id=around(axis, step),
            device_id_type=MESH,
        )
        copy.start()
        copies.append(copy)
    return copies


def pull(level, slot, copies):
    planes, rows, packed, width = level.planes, level.rows, level.packed, level.width
    for copy in copies:
        copy.wait()
    for side, row in ((0, -1), (1, rows)):
        level.v[pl.ds(level.row(slot, 1) + row, planes, stride=level.pitch), :] = level.yrecv[
            pl.ds((slot * 2 + side) * packed, planes), :
        ]
    below = level.zrecv[pl.ds(slot * 2 * rows, rows), :]
    above = level.zrecv[pl.ds((slot * 2 + 1) * rows, rows), :]
    if width < LANES:
        below = pltpu.roll(below, LANES - width, 1)
    above = pltpu.roll(above, width - 2, 1)
    level.edge[...] = jnp.where((lanes_of(rows) & 1) == 0, below, above)


def neighbours(level, slot, plane, center):
    rows, width = level.rows, level.width
    first = level.row(slot, 1) + plane * level.pitch
    at = lambda shift: level.v[pl.ds(first + shift, rows), :]
    lane = lanes_of(rows)
    edge = pltpu.roll(level.edge[...], (LANES - 2 * plane) & (LANES - 1), 1)
    return (
        at(-level.pitch),
        at(level.pitch),
        at(-1),
        at(1),
        jnp.where(lane == 0, edge, pltpu.roll(center, 1, 1)),
        jnp.where(lane == width - 1, edge, pltpu.roll(center, LANES - 1, 1)),
    )


def partial(level, slot, residual):
    rows, planes, flat = level.rows, level.planes, level.planes * level.rows
    held = jnp.zeros((rows, LANES), jnp.float32)
    for plane in range(planes):
        first = level.row(slot, 1) + plane * level.pitch
        at = lambda shift: level.v[pl.ds(first + shift, rows), :]
        off = lambda number: level.off[pl.ds(number * flat + plane * rows, rows), :]
        center = at(0)
        keep = -WEIGHT if residual else 1.0 - WEIGHT
        total = level.rhs[pl.ds(plane * rows, rows), :] + keep * center
        if plane > 0:
            total = total + off(0) * at(-level.pitch)
        if plane < planes - 1:
            total = total + off(1) * at(level.pitch)
        total = total + off(2) * at(-1) + off(3) * at(1)
        total = total + off(4) * pltpu.roll(center, 1, 1) + off(5) * pltpu.roll(center, LANES - 1, 1)
        if residual:
            level.res[pl.ds(plane * rows, rows), :] = total
        else:
            level.v[pl.ds(level.row(1 - slot, 1) + plane * level.pitch, rows), :] = total
            held = pack(level, plane, total, held)
    return held


def arrive(level, slot, copies, ref, base, pitch):
    planes, rows, packed, width = level.planes, level.rows, level.packed, level.width
    flat = planes * rows
    for copy in copies:
        copy.wait()
    for number, plane, there in ((0, 0, 0), (1, planes - 1, planes + 1)):
        at = pl.ds(base + plane * pitch, rows)
        ref[at, :] = ref[at, :] + (
            level.off[pl.ds(number * flat + plane * rows, rows), :]
            * level.v[pl.ds(level.row(slot, there), rows), :]
        )
    for side, row in ((0, 0), (1, rows - 1)):
        at = pl.ds(base + row, planes, stride=pitch)
        ref[at, :] = ref[at, :] + (
            level.yface[pl.ds(side * packed, planes), :]
            * level.yrecv[pl.ds((slot * 2 + side) * packed, planes), :]
        )
    below = level.zrecv[pl.ds(slot * 2 * rows, rows), :]
    above = pltpu.roll(level.zrecv[pl.ds((slot * 2 + 1) * rows, rows), :], width - 2, 1)
    edge = jnp.where((lanes_of(rows) & 1) == 0, below, above) * level.zface[...]
    level.edge[...] = edge
    return edge


def edge_of(level, plane, first, count):
    lane = lanes_of(count)
    shift = (LANES - 2 * plane) & (LANES - 1)
    edge = level.edge[pl.ds(first, count), :]
    moved = pltpu.roll(edge, shift, 1) if shift else edge
    return jnp.where((lane == 0) | (lane == level.width - 1), moved, 0.0)


def close(level, slot, plane, first, count):
    at = pl.ds(level.row(slot, 1) + plane * level.pitch + first, count)
    level.v[at, :] = level.v[at, :] + edge_of(level, plane, first, count)


def join(level, slot, copies, held):
    planes, rows, new = level.planes, level.rows, 1 - slot
    edge = arrive(level, slot, copies, level.v, level.row(new, 1), level.pitch)
    pieces = [(0, 8), (8, rows - 16), (rows - 8, 8)]
    parts = [held[first : first + count] for first, count in pieces]
    for plane in range(planes):
        outer = plane in (0, planes - 1)
        for k, (first, count) in enumerate(pieces):
            if outer or k != 1:
                at = pl.ds(level.row(new, 1) + plane * level.pitch + first, count)
                value = level.v[at, :]
                parts[k] = pack(level, plane, value, parts[k])
                level.v[at, :] = value + edge_of(level, plane, first, count)
    return jnp.concatenate(parts, axis=0) + pltpu.roll(edge, 1, 1)


def rest(level, slot):
    for plane in range(1, level.planes - 1):
        close(level, slot, plane, 8, level.rows - 16)


def complete(level, slot, copies, out):
    rows = level.rows
    arrive(level, slot, copies, level.res, 0, rows)
    for plane in range(level.planes):
        at = pl.ds(plane * rows, rows)
        out[at, :] = (level.res[at, :] + edge_of(level, plane, 0, rows)) * level.diag[at, :]


def smooth(level, slot, held, around, count, between=(), joined=False):
    between = list(between)
    for _ in range(count):
        copies = push(level, slot, held, around)
        if joined:
            rest(level, slot)
        held = partial(level, slot, False)
        if between:
            between.pop(0)()
        held = join(level, slot, copies, held)
        slot, joined = 1 - slot, True
    return slot, held


def restrict(level, read):
    size = level.rows // 2
    for plane in range(level.planes // 2):
        parts = [read(2 * plane + p, q, size) for p in range(2) for q in range(2)]
        level.half[pl.ds(plane * size, size), :] = (parts[0] + parts[1]) + (parts[2] + parts[3])
    row = lax.broadcasted_iota(jnp.int32, (LANES, LANES), 0)
    column = lax.broadcasted_iota(jnp.int32, (LANES, LANES), 1)
    gather = jnp.where((row >> 1) == column, 0.125, 0.0)
    return lax.dot(level.half[...], gather, precision=HIGHEST, preferred_element_type=jnp.float32)


def spread(level, coarse):
    row = lax.broadcasted_iota(jnp.int32, (LANES, LANES), 0)
    column = lax.broadcasted_iota(jnp.int32, (LANES, LANES), 1)
    twice = jnp.where(row == (column >> 1), 1.0, 0.0)
    level.half[...] = lax.dot(coarse, twice, precision=HIGHEST, preferred_element_type=jnp.float32)


def prolong(level, slot, coarse):
    spread(level, coarse)
    size = level.rows // 2
    held = jnp.zeros((level.rows, LANES), jnp.float32)
    for plane in range(level.planes):
        parent = level.half[pl.ds((plane // 2) * size, size), :]
        old, new = level.row(slot, plane + 1), level.row(1 - slot, plane + 1)
        for q in range(2):
            level.v[pl.ds(new + q, size, stride=2), :] = (
                level.v[pl.ds(old + q, size, stride=2), :] + parent
            )
        held = pack(level, plane, level.v[pl.ds(new, level.rows), :], held)
    return held


def coefficients(level, ends):
    rows, planes, width, flat = level.rows, level.planes, level.width, level.planes * level.rows
    lane = lanes_of(rows)
    row = lax.broadcasted_iota(jnp.int32, (rows, LANES), 0)

    never = row < 0
    zface = jnp.zeros((rows, LANES), jnp.float32)
    for plane in range(planes):
        center = level.v[pl.ds(level.row(2, 1) + plane * level.pitch, rows), :]
        outside = (
            ends["gx"][0] if plane == 0 else never,
            ends["gx"][1] if plane == planes - 1 else never,
            (row == 0) & ends["gy"][0],
            (row == rows - 1) & ends["gy"][1],
            (lane == 0) & ends["gz"][0],
            (lane == width - 1) & ends["gz"][1],
        )
        faces = [
            0.5 * (center + jnp.where(out, 0.0, value))
            for out, value in zip(outside, neighbours(level, 2, plane, center), strict=True)
        ]
        diagonal = sum(faces[1:], faces[0])
        inverse = WEIGHT / diagonal
        at = pl.ds(plane * rows, rows)
        level.inverse[at, :] = inverse
        level.diag[at, :] = diagonal * (1.0 / WEIGHT)
        off = [jnp.where(out, 0.0, face * inverse) for out, face in zip(outside, faces, strict=True)]
        level.yface[pl.ds(plane, 1), :] = off[2][:1]
        level.yface[pl.ds(level.packed + plane, 1), :] = off[3][rows - 1 :]
        low = pltpu.roll(off[4], 2 * plane, 1) if plane else off[4]
        high = pltpu.roll(off[5], 2 * plane, 1) if plane else off[5]
        zface = jnp.where(lane == 2 * plane, low, zface)
        zface = jnp.where(lane == ((2 * plane - 1) & (LANES - 1)), high, zface)
        border = (never, never, row == 0, row == rows - 1, lane == 0, lane == width - 1)
        for number in range(6):
            value = off[number] if number < 2 else jnp.where(border[number], 0.0, off[number])
            level.off[pl.ds(number * flat + plane * rows, rows), :] = value
    level.zface[...] = zface


class Wide:
    def __init__(self, index, shape, refs):
        self.index = index
        self.planes, self.rows, self.width = shape
        self.tall = self.rows + 2 * PAD
        self.scale = 0.25**index
        for name, ref in refs.items():
            setattr(self, name, ref)


COEF, RHS, AFTER = 2, 3, 4


def wide_scratch(shape):
    planes, rows, _ = shape
    f32 = jnp.float32
    deep, tall = planes + 2 * HALO, rows + 2 * PAD
    return dict(
        v=pltpu.VMEM((5, deep, tall + 2 * PAD, LANES), f32),
        ends=pltpu.VMEM((3, rows, LANES), f32),
        met=pltpu.VMEM((3, 2, 3, tall, LANES), f32),
        off=pltpu.VMEM((6, deep, tall, LANES), f32),
        inverse=pltpu.VMEM((planes * rows, LANES), f32),
        diag=pltpu.VMEM((planes * rows, LANES), f32),
        res=pltpu.VMEM((planes * rows, LANES), f32),
        half=pltpu.VMEM((planes * rows // 4, LANES), f32),
        send=pltpu.SemaphoreType.DMA((3, 27)),
        recv=pltpu.SemaphoreType.DMA((3, 27)),
    )


def wide_push(level, slot, around):
    planes, rows, width, turn = level.planes, level.rows, level.width, slot - 2
    lane = lanes_of(rows)
    ends = jnp.zeros((rows, LANES), jnp.float32)
    for plane in range(planes):
        low, high = HALO * plane, width - HALO + HALO * plane
        mask = ((lane >= low) & (lane < low + HALO)) | ((lane >= high) & (lane < high + HALO))
        own = level.v[slot, HALO + plane, pl.ds(2 * PAD, rows), :]
        ends = jnp.where(mask, pltpu.roll(own, low, 1) if low else own, ends)
    level.ends[turn] = ends

    def part(step, first, count, size):
        if step == 0:
            return (first, count), (first, count)
        if step > 0:
            return (first + count - size, size), (first - size, size)
        return (first, size), (first + count, size)

    copies = []
    steps = [(a, b, c) for a in (-1, 0, 1) for b in (-1, 0, 1) for c in (-1, 0, 1)]
    for along, across, depth in sorted(steps, key=lambda d: -sum(abs(k) for k in d)):
        (src_x, n_x), (dst_x, _) = part(along, HALO, planes, HALO)
        (src_y, n_y), (dst_y, _) = part(across, PAD, rows, PAD)
        number = (along + 1) * 9 + (across + 1) * 3 + depth + 1
        if number == 13:
            continue
        if depth == 0:
            src = level.v.at[slot, pl.ds(src_x, n_x), pl.ds(PAD + src_y, n_y), :]
            dst = level.v.at[slot, pl.ds(dst_x, n_x), pl.ds(PAD + dst_y, n_y), :]
        else:
            src = level.ends.at[turn, pl.ds(src_y - PAD, n_y), :]
            dst = level.met.at[turn, (1 - depth) // 2, 1 - along, pl.ds(dst_y, n_y), :]
        where = {}
        for axis, step in (("gx", along), ("gy", across), ("gz", depth)):
            if step:
                where.update(around(axis, step))
        copy = pltpu.make_async_remote_copy(
            src_ref=src,
            dst_ref=dst,
            send_sem=level.send.at[turn, number],
            recv_sem=level.recv.at[turn, number],
            device_id=where,
            device_id_type=MESH,
        )
        copy.start()
        copies.append(copy)
    return copies


def wide_pull(level, slot, copies):
    planes, width, tall, turn = level.planes, level.width, level.tall, slot - 2
    lane = lanes_of(tall)
    for copy in copies:
        copy.wait()
    halo = (lane >= LANES - HALO) | ((lane >= width) & (lane < width + HALO))
    for side in range(3):
        below, above = level.met[turn, 0, side], level.met[turn, 1, side]
        if width < LANES // 2:
            below = pltpu.roll(below, LANES - 2 * width, 1)
        both = jnp.where(lane < HALO * planes, above, below)
        first, count, place = (
            (planes - HALO, HALO, 0),
            (0, planes, HALO),
            (0, HALO, HALO + planes),
        )[side]
        for k in range(count):
            shift = (width - HALO * (first + k)) % LANES
            moved = pltpu.roll(both, shift, 1) if shift else both
            old = level.v[slot, place + k, pl.ds(PAD, tall), :]
            level.v[slot, place + k, pl.ds(PAD, tall), :] = jnp.where(halo, moved, old)


def wide_neighbours(level, slot, plane, first, rows):
    at = lambda p, r: level.v[slot, p, pl.ds(r, rows), :]
    center = at(plane, first)
    return center, (
        at(plane - 1, first),
        at(plane + 1, first),
        at(plane, first - 1),
        at(plane, first + 1),
        pltpu.roll(center, 1, 1),
        pltpu.roll(center, LANES - 1, 1),
    )


def wide_change(level, slot, plane, first, rows):
    center, values = wide_neighbours(level, slot, plane, first, rows)
    total = level.v[RHS, plane, pl.ds(first, rows), :] - WEIGHT * center
    for number, value in enumerate(values):
        total = total + level.off[number, plane, pl.ds(first - PAD, rows), :] * value
    return center, total


def wide_sweep(level, slot, into, layers):
    for plane in range(HALO - layers, HALO + level.planes + layers):
        center, total = wide_change(level, slot, plane, PAD, level.tall)
        level.v[into, plane, pl.ds(PAD, level.tall), :] = center + total


def wide_residual(level, slot):
    for plane in range(level.planes):
        at = pl.ds(plane * level.rows, level.rows)
        total = wide_change(level, slot, HALO + plane, 2 * PAD, level.rows)[1]
        level.res[at, :] = total * level.diag[at, :]


def wide_put(level, slot, values):
    for plane in range(level.planes):
        level.v[slot, HALO + plane, pl.ds(2 * PAD, level.rows), :] = values[
            plane * level.rows : (plane + 1) * level.rows, :
        ]


def wide_prolong(level, slot, into, coarse):
    spread(level, coarse)
    size = level.rows // 2
    for plane in range(level.planes):
        parent = level.half[pl.ds((plane // 2) * size, size), :]
        for q in range(2):
            at = pl.ds(2 * PAD + q, size, stride=2)
            level.v[into, HALO + plane, at, :] = level.v[slot, HALO + plane, at, :] + parent


def wide_own(level, slot):
    inside = lanes_of(level.rows) < level.width
    own = [
        jnp.where(inside, level.v[slot, HALO + plane, pl.ds(2 * PAD, level.rows), :], 0.0)
        for plane in range(level.planes)
    ]
    return jnp.concatenate(own, axis=0)


def wide_coefficients(level, ends):
    rows, tall, planes, width = level.rows, level.tall, level.planes, level.width
    lane = lanes_of(tall)
    row = lax.broadcasted_iota(jnp.int32, (tall, LANES), 0)
    never = row < 0
    known = (lane < width + HALO) | (lane >= LANES - HALO)
    inside = lanes_of(rows) < width
    for plane in range(1, planes + 2 * HALO - 1):
        center, values = wide_neighbours(level, COEF, plane, PAD, tall)
        outside = (
            ends["gx"][0] if plane == HALO else never,
            ends["gx"][1] if plane == HALO + planes - 1 else never,
            (row == PAD) & ends["gy"][0],
            (row == PAD + rows - 1) & ends["gy"][1],
            (lane == 0) & ends["gz"][0],
            (lane == width - 1) & ends["gz"][1],
        )
        faces = [
            0.5 * (center + jnp.where(out, 0.0, value))
            for out, value in zip(outside, values, strict=True)
        ]
        diagonal = sum(faces[1:], faces[0])
        inverse = jnp.where(known, WEIGHT / diagonal, 0.0)
        for number in range(6):
            level.off[number, plane] = jnp.where(outside[number], 0.0, faces[number] * inverse)
        if HALO <= plane < HALO + planes:
            at = pl.ds((plane - HALO) * rows, rows)
            own = slice(PAD, PAD + rows)
            level.inverse[at, :] = jnp.where(inside, inverse[own] * (1.0 / level.scale), 0.0)
            level.diag[at, :] = jnp.where(inside, diagonal[own] * (level.scale / WEIGHT), 0.0)


def gather_ring(field, which, co, place, around):
    rows = field.shape[0] // 2
    tile = pltpu.roll(field[:rows, :], place["lane"], 1) + pltpu.roll(
        field[rows:, :], place["lane"] + LANES // 2, 1
    )
    co["tile"][pl.ds(which * 8, 8), :] = tile
    copies = []
    for step in range(1, place["count"]["gz"]):
        copy = pltpu.make_async_remote_copy(
            src_ref=co["tile"].at[pl.ds(which * 8, 8), :],
            dst_ref=co["tiles"].at[pl.ds((which * 4 + step) * 8, 8), :],
            send_sem=co["ring_send"].at[which, step],
            recv_sem=co["ring_recv"].at[which, step],
            device_id=around("gz", step),
            device_id_type=MESH,
        )
        copy.start()
        copies.append(copy)
    return tile, copies


def gather_plane(tile, copies, which, co, place, around):
    for copy in copies:
        copy.wait()
    for step in range(1, place["count"]["gz"]):
        tile = tile + co["tiles"][pl.ds((which * 4 + step) * 8, 8), :]
    mine = co["whole"].at[which, pl.ds(place["row"], 8), :]
    mine[...] = tile
    gx, gy = place["count"]["gx"], place["count"]["gy"]
    others = [(along, across) for along in range(gx) for across in range(gy) if along or across]
    far = lambda step: min(step[0], gx - step[0]) + 2 * min(step[1], gy - step[1])
    for along, across in sorted(others, key=lambda step: -far(step)):
        pltpu.make_async_remote_copy(
            src_ref=mine,
            dst_ref=mine,
            send_sem=co["plane_send"].at[which],
            recv_sem=co["plane_recv"].at[which],
            device_id={**around("gx", along), **around("gy", across)},
            device_id_type=MESH,
        ).start()


def gather_wait(which, co):
    total = co["whole"].shape[1]
    others = co["whole"].at[which, pl.ds(0, total - 8), :]
    pltpu.make_async_copy(others, others, co["plane_send"].at[which]).wait()
    pltpu.make_async_copy(others, others, co["plane_recv"].at[which]).wait()


def coarse_solve(co, scale):
    total = co["whole"].shape[1]
    count, rows = co["whole"].shape[1] // 32, 32
    lane = lanes_of(rows)
    row = lax.broadcasted_iota(jnp.int32, (rows, LANES), 0)
    low = lane < LANES // 2
    depth = lane & (LANES // 2 - 1)

    def around_of(read, group):
        center = read(group)
        swap = lambda g: pltpu.roll(read(g), LANES // 2, 1)
        here = swap(group)
        before = swap(group - 1) if group > 0 else here
        after = swap(group + 1) if group < count - 1 else here
        return center, (
            jnp.where(low, before, here),
            jnp.where(low, here, after),
            pltpu.roll(center, 1, 0),
            pltpu.roll(center, rows - 1, 0),
            pltpu.roll(center, 1, 1),
            pltpu.roll(center, LANES - 1, 1),
        )

    read_coef = lambda g: co["whole"][0, pl.ds(g * rows, rows), :]
    for group in range(count):
        center, values = around_of(read_coef, group)
        never = row < 0
        outside = (
            low if group == 0 else never,
            ~low if group == count - 1 else never,
            row == 0,
            row == rows - 1,
            depth == 0,
            depth == LANES // 2 - 1,
        )
        faces = [
            0.5 * (center + jnp.where(out, 0.0, value))
            for out, value in zip(outside, values, strict=True)
        ]
        diagonal = sum(faces[1:], faces[0])
        inverse = WEIGHT / diagonal
        at = pl.ds(group * rows, rows)
        for number in range(6):
            co["off"][number, at, :] = jnp.where(outside[number], 0.0, faces[number] * inverse)
        co["inverse"][at, :] = inverse * (1.0 / scale)

    yield

    start = co["whole"][1] * co["inverse"][...]
    co["inverse"][...] = start
    co["v"][0] = jnp.zeros((total + 2 * MARGIN, LANES), jnp.float32)

    def one(slot):
        read = lambda g: co["v"][slot, pl.ds(MARGIN + g * rows, rows), :]
        for group in range(count):
            center, values = around_of(read, group)
            at = pl.ds(group * rows, rows)
            new = co["inverse"][at, :] + (1.0 - WEIGHT) * center
            for number, value in enumerate(values):
                new = new + co["off"][number, at, :] * value
            co["v"][1 - slot, pl.ds(MARGIN + group * rows, rows), :] = new

    def pair(_, carry):
        one(0)
        one(1)
        return carry

    lax.fori_loop(0, COARSE // 2, pair, 0)


def kernel(shapes, counts, table_in, source_in, guess_in, classes_in, out_u, out_r, refs, co, got):
    table, source, guess, classes = got["table"], got["source"], got["guess"], got["classes"]
    arriving = [
        pltpu.make_async_copy(src, dst, got["sem"].at[number])
        for number, (src, dst) in enumerate(
            ((table_in, table), (classes_in, classes), (guess_in, guess), (source_in, source))
        )
    ]
    for copy in arriving:
        copy.start()
    top = Level(0, shapes[0], refs[0])
    lower = [Wide(index, shapes[index], refs[index]) for index in range(1, len(shapes))]
    position = {axis: lax.axis_index(axis) for axis in counts}

    def around(axis, step):
        count = counts[axis]
        return {axis: lax.rem(position[axis] + (step + count), count)}

    ends = {axis: (position[axis] == 0, position[axis] == counts[axis] - 1) for axis in counts}
    piece = shapes[-1][2] // 2
    place = dict(
        count=counts,
        lane=position["gz"] * piece,
        row=pl.multiple_of(position["gx"] * 32 + position["gy"] * 8, 8),
    )

    partners = [(axis, step) for axis in counts for step in (-1, 1)]
    barrier = pltpu.get_barrier_semaphore()
    for axis, step in partners:
        pl.semaphore_signal(barrier, inc=1, device_id=around(axis, step), device_id_type=MESH)

    for row in (top.row(0, 1) - 1, top.row(0, 1) + top.rows, top.row(1, 1) - 1, top.row(1, 1) + top.rows):
        top.v[pl.ds(row, top.planes, stride=top.pitch), :] = jnp.zeros((top.planes, LANES), jnp.float32)
    for copy in arriving[:3]:
        copy.wait()
    entries = [table[k] for k in range(8)]
    held_c = held_v = jnp.zeros((top.rows, LANES), jnp.float32)
    for plane in range(top.planes):
        at = pl.ds(plane * top.rows, top.rows)
        kind = classes[at, :]
        pick = entries
        for k in range(3):
            bit = (kind & (1 << k)) != 0
            pick = [jnp.where(bit, pick[2 * m + 1], pick[2 * m]) for m in range(len(pick) // 2)]
        values = guess[at, :]
        top.v[pl.ds(top.row(2, 1) + plane * top.pitch, top.rows), :] = pick[0]
        top.v[pl.ds(top.row(0, 1) + plane * top.pitch, top.rows), :] = values
        held_c = pack(top, plane, pick[0], held_c)
        held_v = pack(top, plane, values, held_v)
    pl.semaphore_wait(barrier, len(partners))

    moving = push(top, 2, held_c, around)
    first = push(top, 0, held_v, around)
    coarse = restrict(
        top, lambda plane, q, n: top.v[pl.ds(top.row(2, 1) + plane * top.pitch + q, n, stride=2), :]
    )
    for level in lower:
        wide_put(level, COEF, coarse)
        coarse = restrict(
            level,
            lambda plane, q, n: level.v[COEF, HALO + plane, pl.ds(2 * PAD + q, n, stride=2), :],
        )
    pull(top, 2, moving)
    tile, ring = gather_ring(coarse, 0, co, place, around)
    coefficients(top, ends)
    arriving[3].wait()
    top.rhs[...] = source[...] * top.inverse[...]
    held = join(top, 0, first, partial(top, 0, False))

    wide_moving = {}

    def depart():
        for level in lower:
            wide_moving[level.index] = wide_push(level, COEF, around)

    def ready(level):
        wide_pull(level, COEF, wide_moving[level.index])
        wide_coefficients(level, ends)

    solve = coarse_solve(co, 0.25**LEVELS)

    def ready_coarse():
        gather_wait(0, co)
        next(solve)

    between = [lambda: None, depart, functools.partial(ready, lower[0])]
    slot, held = smooth(top, 1, held, around, SWEEPS - 1, between, joined=True)
    copies = push(top, slot, held, around)
    rest(top, slot)
    partial(top, slot, True)
    for level in lower[1:]:
        ready(level)
    complete(top, slot, copies, top.res)
    fine = slot
    rhs = restrict(top, lambda plane, q, n: top.res[pl.ds(plane * top.rows + q, n, stride=2), :])
    for level in lower:
        wide_put(level, RHS, rhs * level.inverse[...])
        copies = wide_push(level, RHS, around)
        if level is lower[0]:
            gather_plane(tile, ring, 0, co, place, around)
        if level is lower[-1]:
            ready_coarse()
        wide_pull(level, RHS, copies)
        slot = RHS
        for count in range(SWEEPS - 1):
            wide_sweep(level, slot, count % 2, HALO - 1 - count)
            slot = count % 2
        wide_residual(level, slot)
        rhs = restrict(
            level, lambda plane, q, n: level.res[pl.ds(plane * level.rows + q, n, stride=2), :]
        )

    tile, copies = gather_ring(rhs, 1, co, place, around)
    last = lower[-1]
    wide_put(last, AFTER, wide_own(last, (SWEEPS - 2) % 2))
    wide_moving[0] = wide_push(last, AFTER, around)
    gather_plane(tile, copies, 1, co, place, around)
    gather_wait(1, co)
    next(solve, None)

    wide_pull(last, AFTER, wide_moving[0])
    tall = last.tall // 2
    lane = lanes_of(tall)
    inside = (lane < piece + HALO // 2) | (lane >= LANES - HALO // 2)
    back = LANES - place["lane"]
    parents = []
    for group in (-1, 0, 1):
        start = place["row"] + (MARGIN + group * 32 - PAD // 2)
        mine = co["v"][0, pl.ds(start, tall), :]
        for half in range(2):
            moved = pltpu.roll(mine, (back + half * (LANES // 2)) & (LANES - 1), 1)
            parents.append(jnp.where(inside, moved, 0.0))
    row = lax.broadcasted_iota(jnp.int32, (LANES, LANES), 0)
    column = lax.broadcasted_iota(jnp.int32, (LANES, LANES), 1)
    source_lane = jnp.where(column >= LANES - HALO, (column >> 1) + LANES // 2, column >> 1)
    twice = jnp.where(row == source_lane, 1.0, 0.0)
    parents = lax.dot(
        jnp.concatenate(parents, axis=0), twice, precision=HIGHEST, preferred_element_type=jnp.float32
    )
    for plane in range(last.planes + 2 * HALO):
        parent = parents[(plane // 2) * tall : (plane // 2 + 1) * tall]
        for q in range(2):
            at = pl.ds(PAD + q, tall, stride=2)
            last.v[AFTER, plane, at, :] = last.v[AFTER, plane, at, :] + parent
    for level in reversed(lower):
        if level is not last:
            wide_prolong(level, (SWEEPS - 2) % 2, AFTER, coarse)
            wide_pull(level, AFTER, wide_push(level, AFTER, around))
        slot = AFTER
        for count in range(SWEEPS):
            wide_sweep(level, slot, count % 2, HALO - 1 - count)
            slot = count % 2
        coarse = wide_own(level, slot)
    held = prolong(top, fine, coarse)
    slot, held = smooth(top, 1 - fine, held, around, SWEEPS)
    copies = push(top, slot, held, around)
    rest(top, slot)
    for plane in range(top.planes):
        out_u[pl.ds(plane * top.rows, top.rows), :] = top.v[pl.ds(top.row(slot, plane + 1), top.rows), :]
    partial(top, slot, True)
    complete(top, slot, copies, out_r)


def body(counts, source, first_guess, cell_classes, class_table):
    planes, rows, width = source.shape
    shapes = [(planes >> k, rows >> k, width >> k) for k in range(LEVELS)]
    flat = (planes * rows, width)
    whole = counts["gx"] * 32
    f32 = jnp.float32
    co = dict(
        tile=pltpu.VMEM((2 * 8, LANES), f32),
        tiles=pltpu.VMEM((2 * 4 * 8, LANES), f32),
        whole=pltpu.VMEM((2, whole, LANES), f32),
        off=pltpu.VMEM((6, whole, LANES), f32),
        inverse=pltpu.VMEM((whole, LANES), f32),
        v=pltpu.VMEM((2, whole + 2 * MARGIN, LANES), f32),
        ring_send=pltpu.SemaphoreType.DMA((2, 4)),
        ring_recv=pltpu.SemaphoreType.DMA((2, 4)),
        plane_send=pltpu.SemaphoreType.DMA((2,)),
        plane_recv=pltpu.SemaphoreType.DMA((2,)),
    )
    got = dict(
        table=pltpu.SMEM(class_table.shape, f32),
        source=pltpu.VMEM(flat, f32),
        guess=pltpu.VMEM(flat, f32),
        classes=pltpu.VMEM(flat, jnp.int32),
        sem=pltpu.SemaphoreType.DMA((4,)),
    )
    vmem = pl.BlockSpec(memory_space=pltpu.VMEM)
    solution_out, residual_out = pl.pallas_call(
        functools.partial(kernel, shapes, counts),
        out_shape=[jax.ShapeDtypeStruct(flat, f32)] * 2,
        in_specs=[pl.BlockSpec(memory_space=pltpu.HBM)] * 4,
        out_specs=[vmem, vmem],
        scratch_shapes=[[level_scratch(shapes[0])] + [wide_scratch(shape) for shape in shapes[1:]], co, got],
        compiler_params=pltpu.CompilerParams(
            collective_id=0, has_side_effects=True, vmem_limit_bytes=VMEM_BYTES
        ),
        cost_estimate=pl.CostEstimate(flops=100_000_000, bytes_accessed=3_000_000, transcendentals=0),
        name="vcycle",
    )(class_table, source.reshape(flat), first_guess.reshape(flat), cell_classes.reshape(flat))
    return solution_out.reshape(source.shape), residual_out.reshape(source.shape)


def solution(mesh):
    counts = {axis: mesh.shape[axis] for axis in ("gx", "gy", "gz")}
    spec = P("gx", "gy", "gz")
    return jax.shard_map(
        functools.partial(body, counts),
        mesh=mesh,
        in_specs=(spec, spec, spec, P()),
        out_specs=(spec, spec),
        check_vma=False,
    )
```
